256 devices in a mesh: dp: 4 (over x), section: 2 (over z_hi), shard: 32 (over z_lo, y, core).
Axes of the slice: x: 4, y: 4, z: 8 (z_hi: 2, z_lo: 4; z = z_hi * 4 + z_lo), core: 2. Of those that a mesh axis runs over, the one named last changes fastest.
Arguments:
- projections: bfloat16 [2, 8, 2048, 3, 4096], P('section', 'dp', 'shard'), may hold values from -40 to 40
- bias_terms: float32 [3, 4096], replicated, may hold values from -3 to 3
- context_grad: bfloat16 [2, 4, 32, 1, 2048, 256], P('section', 'dp', 'shard'), may hold values from -20 to 20
Outputs:
- context: bfloat16 [2, 4, 32, 1, 2048, 256], P('section', 'dp', 'shard')
- projection_grad: bfloat16 [2, 8, 2048, 3, 4096], P('section', 'dp', 'shard')
- bias_grad: float32 [3, 4096], replicated
The draws below stay inside these ranges and needn't reach their ends.
All inputs are finite; a program needn't handle non-finite values.
Results may differ from the reference program's by a relative error of at most 0.012.
The reference program's roundings to bfloat16 on the way count: a program that leaves them out, or rounds other values in their place, can miss the bound.
Values may be sent and summed in bfloat16 or wider, within the bound.
A program may use at most 128 MiB of HBM per device.

```python
import jax
import jax.numpy as jnp
from jax import lax

HEAD_DIM = 128
HEAD_DEV = 2
SEQ_LEN = 2048
BATCH = 2
HEADS = 32
WIDTH = 4096
N_DP = 4
N_SECTION = 2
N_SHARD = 32


def draw_projections(key, part):
    key = jax.random.fold_in(key, 7)
    full_shape = (N_SECTION, N_DP * BATCH, SEQ_LEN, 3, WIDTH)
    return jax.random.truncated_normal(key, -6.0, 6.0, full_shape, jnp.float32).astype(jnp.bfloat16)


def draw_context_grad(key, part):
    key = jax.random.fold_in(key, 13)
    full_shape = (N_SECTION, N_DP, N_SHARD, BATCH // 2, SEQ_LEN, HEAD_DEV * HEAD_DIM)
    position_ramp = 1.0 + 2.0 * lax.broadcasted_iota(jnp.float32, full_shape, 4) / SEQ_LEN
    sampled = jax.random.truncated_normal(key, -6.0, 6.0, full_shape, jnp.float32)
    return (sampled * position_ramp).astype(jnp.bfloat16)


def gaussian(own_key, extent, scale, bound, held_as=jnp.bfloat16):
    return jnp.clip(scale * jax.random.normal(own_key, extent, jnp.float32), -bound, bound).astype(held_as)


def setup_inputs(seed: int = 0) -> dict:
    streams_of = jax.random.split(jax.random.key(seed), 4)
    projections = draw_projections(jax.random.fold_in(streams_of[3], 71), 0)
    bias_terms = gaussian(streams_of[1], (3, WIDTH), 0.5, 3.0, jnp.float32)
    context_grad = draw_context_grad(jax.random.fold_in(streams_of[3], 71), 0)
    return {"projections": projections, "bias_terms": bias_terms, "context_grad": context_grad}


def attend_pair(inputs):
    query, keyed, valued, grad_out = inputs
    length = query.shape[0]
    score_scale = HEAD_DIM ** -0.5
    scores = jnp.dot(query, keyed.T, preferred_element_type=jnp.float32) * score_scale
    row_ids = lax.broadcasted_iota(jnp.int32, (length, length), 0)
    col_ids = lax.broadcasted_iota(jnp.int32, (length, length), 1)
    scores = jnp.where(col_ids <= row_ids, scores, -jnp.inf)
    row_top = jnp.max(scores, axis=1, keepdims=True)
    exponent = jnp.exp(scores - row_top)
    probability = exponent / jnp.sum(exponent, axis=1, keepdims=True)
    weights = probability.astype(jnp.bfloat16)
    context = jnp.dot(weights, valued, preferred_element_type=jnp.float32).astype(jnp.bfloat16)
    grad_prob = jnp.dot(grad_out, valued.T, preferred_element_type=jnp.float32)
    row_delta = jnp.sum(probability * grad_prob, axis=1, keepdims=True)
    grad_score = (probability * (grad_prob - row_delta) * score_scale).astype(jnp.bfloat16)
    grad_query = jnp.dot(grad_score, keyed, preferred_element_type=jnp.float32).astype(jnp.bfloat16)
    grad_key = jnp.dot(grad_score.T, query, preferred_element_type=jnp.float32).astype(jnp.bfloat16)
    grad_value = jnp.dot(weights.T, grad_out, preferred_element_type=jnp.float32).astype(jnp.bfloat16)
    return context, grad_query, grad_key, grad_value


def reference(projections, bias_terms, context_grad):
    sections, replicas_batch, length, triple, width_all = projections.shape
    groups = N_SHARD // 2
    half_batch = BATCH // 2
    head_width = HEAD_DEV * HEAD_DIM
    biased = (projections.astype(jnp.float32) + bias_terms).astype(jnp.bfloat16)

    def to_items(tensor):
        shaped = tensor.reshape(sections * replicas_batch, length, HEADS, HEAD_DIM)
        return shaped.transpose(0, 2, 1, 3).reshape(sections * replicas_batch * HEADS, length, HEAD_DIM)

    def from_items(items):
        shaped = items.reshape(sections * replicas_batch, HEADS, length, HEAD_DIM)
        return shaped.transpose(0, 2, 1, 3).reshape(sections, replicas_batch, length, width_all)

    natural_grad = jnp.flip(context_grad, axis=0).reshape(sections, N_DP, 2, groups, half_batch, length, head_width)
    natural_grad = natural_grad.transpose(0, 1, 2, 4, 5, 3, 6).reshape(sections, replicas_batch, length, width_all)
    outputs = lax.map(attend_pair, (to_items(biased[:, :, :, 0]), to_items(biased[:, :, :, 1]),
                                    to_items(biased[:, :, :, 2]), to_items(natural_grad)))
    context_nat = from_items(outputs[0]).reshape(sections, N_DP, 2, half_batch, length, groups, head_width)
    context_nat = context_nat.transpose(0, 1, 2, 5, 3, 4, 6).reshape(sections, N_DP, N_SHARD, half_batch, length, head_width)
    context = jnp.flip(context_nat, axis=0)
    projection_grad = jnp.stack([from_items(outputs[1]), from_items(outputs[2]), from_items(outputs[3])], axis=3)
    bias_grad = jnp.sum(projection_grad.astype(jnp.float32), axis=(0, 1, 2))
    return context, projection_grad, bias_grad
```

```python
import functools

import jax
import jax.numpy as jnp
from jax import lax
from jax.experimental import pallas as pl
from jax.experimental.pallas import tpu as pltpu
from jax.sharding import PartitionSpec as P

HEAD_DIM = 128
N_Z, N_Y, N_CORE = 4, 4, 2
N_SHARD = N_Z * N_Y * N_CORE
LINE = N_Y * N_CORE
PIECE = 64
SEQ_LEN = N_SHARD * PIECE
WIDTH = 4096
BLOCK = 512
N_BLOCK = SEQ_LEN // BLOCK
MESH = pl.DeviceIdType.MESH


def kernel(
    proj_ref, bias_ref, cot_ref, context_ref, grad_ref, bias_grad_ref,
    biased, qkv, cot, ctx, grads, dk_acc, dv_acc, ctx_acc, dq_acc, score, dprob, k_t, v_t,
    part, total, stage1, stage2,
    in_send, in_recv, cot_send, cot_recv, out_send, out_recv, ctx_send, ctx_recv,
    s1_send, s1_recv, s2_send, s2_recv,
):
    dp = lax.axis_index("dp")
    section = lax.axis_index("section")
    me = lax.axis_index("shard")
    z, inner = me // LINE, me % LINE
    y, core = inner // N_CORE, inner % N_CORE
    partner = (dp, 1 - section, (N_Z - 1 - z) * LINE + inner)
    scale = HEAD_DIM ** -0.5

    def peer(step):
        to_z = (z + step % N_Z) % N_Z
        rest = step // N_Z
        to_y = (y + rest // N_CORE) % N_Y
        to_core = (core + rest % N_CORE) % N_CORE
        return to_z * LINE + to_y * N_CORE + to_core

    def held_by(shard):
        home = (N_Z - 1 - shard // LINE) * LINE + shard % LINE
        return home // (N_SHARD // 2), (home % (N_SHARD // 2)) * 2

    def same_heads(step):
        return (dp + step // 4) % 4, (section + step // 2 % 2) % 2, ((z // 2 + step % 2) % 2) * 2 + z % 2

    def all_heads(step):
        to_z = z // 2 * 2 + (z % 2 + step // LINE) % 2
        to_y = (y + step % LINE // N_CORE) % N_Y
        to_core = (core + step % N_CORE) % N_CORE
        return to_z * LINE + to_y * N_CORE + to_core

    barrier = pltpu.get_barrier_semaphore()

    def greet_section(step, carry):
        pl.semaphore_signal(barrier, inc=1, device_id=(dp, section, peer(step)), device_id_type=MESH)
        return carry

    lax.fori_loop(1, N_SHARD, greet_section, 0)
    pl.semaphore_signal(barrier, inc=1, device_id=partner, device_id_type=MESH)

    def greet_group(step, carry):
        to_dp, to_section, to_z = same_heads(step)
        pl.semaphore_signal(
            barrier, inc=1, device_id=(to_dp, to_section, to_z * LINE + inner), device_id_type=MESH
        )
        return carry

    lax.fori_loop(2, 16, greet_group, 0)

    for n in range(2):
        for kind in range(3):
            biased[n, kind] = (
                proj_ref[n, kind].astype(jnp.float32) + bias_ref[kind:kind + 1, :]
            ).astype(jnp.bfloat16)

    pl.semaphore_wait(barrier, N_SHARD - 1 + 1 + 14)

    my_seq, my_head = held_by(me)
    my_rows = pl.ds(pl.multiple_of(me * PIECE, PIECE), PIECE)

    def columns(head):
        return pl.ds(pl.multiple_of(head * HEAD_DIM, HEAD_DIM), HEAD_DIM)

    def in_copy(step, h):
        to = peer(step)
        seq, head = held_by(to)
        return pltpu.make_async_remote_copy(
            src_ref=biased.at[seq, :, :, columns(head + h)],
            dst_ref=qkv.at[h, :, my_rows, :],
            send_sem=in_send.at[h, step],
            recv_sem=in_recv.at[h],
            device_id=(dp, section, to),
            device_id_type=MESH,
        )

    def out_copy(step, h):
        to = peer(step)
        rows = pl.ds(pl.multiple_of(to * PIECE, PIECE), PIECE)
        return pltpu.make_async_remote_copy(
            src_ref=grads.at[h, :, rows, :],
            dst_ref=grad_ref.at[my_seq, :, :, columns(my_head + h)],
            send_sem=out_send.at[h, step],
            recv_sem=out_recv,
            device_id=(dp, section, to),
            device_id_type=MESH,
        )

    def cot_copy(h):
        return pltpu.make_async_remote_copy(
            src_ref=cot_ref.at[:, columns(h)],
            dst_ref=cot.at[h],
            send_sem=cot_send.at[h],
            recv_sem=cot_recv.at[h],
            device_id=partner,
            device_id_type=MESH,
        )

    def ctx_copy(h):
        return pltpu.make_async_remote_copy(
            src_ref=ctx.at[h],
            dst_ref=context_ref.at[:, columns(h)],
            send_sem=ctx_send.at[h],
            recv_sem=ctx_recv.at[h],
            device_id=partner,
            device_id_type=MESH,
        )

    def start_in(step, carry):
        in_copy(step, 0).start()
        return carry

    for h in range(2):
        pltpu.make_async_copy(
            biased.at[my_seq, :, :, columns(my_head + h)], qkv.at[h, :, my_rows, :], in_recv.at[h]
        ).start()
    cot_copy(0).start()
    lax.fori_loop(1, N_SHARD, start_in, 0)

    def follow_in(step, carry):
        in_copy(step, 0).wait_send()
        in_copy(step, 1).start()
        return carry

    lax.fori_loop(1, N_SHARD, follow_in, 0)
    cot_copy(1).start()

    part[...] = jnp.zeros_like(part)

    def rows_of(block):
        return pl.ds(pl.multiple_of(block * BLOCK, BLOCK), BLOCK)

    def head_step(h, carry):
        pltpu.make_async_copy(qkv.at[h], qkv.at[h], in_recv.at[h]).wait()

        def turn(c, carry):
            k_t[:, rows_of(c)] = qkv[h, 1, rows_of(c), :].T
            v_t[:, rows_of(c)] = qkv[h, 2, rows_of(c), :].T
            return carry

        lax.fori_loop(0, N_BLOCK, turn, 0)
        dk_acc[...] = jnp.zeros_like(dk_acc)
        dv_acc[...] = jnp.zeros_like(dv_acc)
        cot_copy(h).wait_recv()

        def query_block(b, carry):
            query = qkv[h, 0, rows_of(b), :]
            grad_out = cot[h, rows_of(b), :]
            ctx_acc[...] = jnp.zeros_like(ctx_acc)
            dq_acc[...] = jnp.zeros_like(dq_acc)

            def scores_of(c):
                return lax.dot_general(
                    qkv[h, 1, rows_of(c), :], query, (((1,), (1,)), ((), ())),
                    preferred_element_type=jnp.float32,
                ) * scale

            def first(c, top):
                s = scores_of(c)
                score[rows_of(c), :] = s
                return jnp.maximum(top, jnp.max(s, axis=0, keepdims=True))

            top = lax.fori_loop(0, b, first, jnp.full((1, BLOCK), -jnp.inf, jnp.float32))
            s = scores_of(b)
            key_id = lax.broadcasted_iota(jnp.int32, s.shape, 0)
            query_id = lax.broadcasted_iota(jnp.int32, s.shape, 1)
            s = jnp.where(key_id <= query_id, s, -jnp.inf)
            score[rows_of(b), :] = s
            top = jnp.maximum(top, jnp.max(s, axis=0, keepdims=True))

            def second(c, denom):
                e = jnp.exp(score[rows_of(c), :] - top)
                score[rows_of(c), :] = e
                return denom + jnp.sum(e, axis=0, keepdims=True)

            denom = lax.fori_loop(0, b + 1, second, jnp.zeros((1, BLOCK), jnp.float32))
            inverse = 1.0 / denom

            def third(c, delta):
                probability = score[rows_of(c), :] * inverse
                weights = probability.astype(jnp.bfloat16)
                ctx_acc[...] += jnp.dot(v_t[:, rows_of(c)], weights, preferred_element_type=jnp.float32)
                dv_acc[rows_of(c), :] += jnp.dot(weights, grad_out, preferred_element_type=jnp.float32)
                grad_prob = lax.dot_general(
                    qkv[h, 2, rows_of(c), :], grad_out, (((1,), (1,)), ((), ())),
                    preferred_element_type=jnp.float32,
                )
                dprob[rows_of(c), :] = grad_prob
                return delta + jnp.sum(probability * grad_prob, axis=0, keepdims=True)

            delta = lax.fori_loop(0, b + 1, third, jnp.zeros((1, BLOCK), jnp.float32))

            def fourth(c, carry):
                probability = score[rows_of(c), :] * inverse
                grad_score = (probability * (dprob[rows_of(c), :] - delta) * scale).astype(jnp.bfloat16)
                dq_acc[...] += jnp.dot(k_t[:, rows_of(c)], grad_score, preferred_element_type=jnp.float32)
                dk_acc[rows_of(c), :] += jnp.dot(grad_score, query, preferred_element_type=jnp.float32)
                return carry

            lax.fori_loop(0, b + 1, fourth, 0)
            ctx[h, rows_of(b), :] = ctx_acc[...].T.astype(jnp.bfloat16)
            grads[h, 0, rows_of(b), :] = dq_acc[...].T.astype(jnp.bfloat16)
            return carry

        lax.fori_loop(0, N_BLOCK, query_block, 0)
        ctx_copy(h).start()

        def finish(c, carry):
            dk = dk_acc[rows_of(c), :].astype(jnp.bfloat16)
            dv = dv_acc[rows_of(c), :].astype(jnp.bfloat16)
            grads[h, 1, rows_of(c), :] = dk
            grads[h, 2, rows_of(c), :] = dv
            dq = grads[h, 0, rows_of(c), :]
            return tuple(
                acc + jnp.sum(x.astype(jnp.float32), axis=0, keepdims=True)
                for acc, x in zip(carry, (dq, dk, dv))
            )

        sums = lax.fori_loop(0, N_BLOCK, finish, (jnp.zeros((1, HEAD_DIM), jnp.float32),) * 3)
        for kind in range(3):
            part[h, kind:kind + 1, :] = sums[kind]

        own = pltpu.make_async_copy(
            grads.at[h, :, my_rows, :], grad_ref.at[my_seq, :, :, columns(my_head + h)], out_recv
        )
        own.start()

        def start_out(step, carry):
            out_copy(step, h).start()
            return carry

        lax.fori_loop(1, N_SHARD, start_out, 0)
        return carry

    lax.fori_loop(0, 2, head_step, 0)

    group = (dp * 2 + section) * 2 + z // 2
    pair = my_head // 2

    def s1_copy(step):
        to_dp, to_section, to_z = same_heads(step)
        return pltpu.make_async_remote_copy(
            src_ref=part, dst_ref=stage1.at[group], send_sem=s1_send.at[step], recv_sem=s1_recv,
            device_id=(to_dp, to_section, to_z * LINE + inner), device_id_type=MESH,
        )

    def s2_copy(step):
        return pltpu.make_async_remote_copy(
            src_ref=total, dst_ref=stage2.at[pair], send_sem=s2_send.at[step], recv_sem=s2_recv,
            device_id=(dp, section, all_heads(step)), device_id_type=MESH,
        )

    def run(make, method):
        def body(step, carry):
            getattr(make(step), method)()
            return carry
        lax.fori_loop(1, 16, body, 0)

    pltpu.make_async_copy(part, stage1.at[group], s1_recv).start()
    run(s1_copy, "start")
    pltpu.make_async_copy(stage1, stage1, s1_recv).wait()
    total[...] = jnp.sum(stage1[...], axis=0)
    pltpu.make_async_copy(total, stage2.at[pair], s2_recv).start()
    run(s2_copy, "start")
    pltpu.make_async_copy(stage2, stage2, s2_recv).wait()
    for p in range(16):
        for h in range(2):
            first_column = (p * 2 + h) * HEAD_DIM
            bias_grad_ref[:, first_column:first_column + HEAD_DIM] = stage2[p, h, 0:3, :]
    run(s1_copy, "wait_send")
    run(s2_copy, "wait_send")

    def drain(step, carry):
        in_copy(step, 1).wait_send()
        out_copy(step, 0).wait_send()
        out_copy(step, 1).wait_send()
        return carry

    lax.fori_loop(1, N_SHARD, drain, 0)
    for h in range(2):
        cot_copy(h).wait_send()
        ctx_copy(h).wait_send()
        ctx_copy(h).wait_recv()
    pltpu.make_async_copy(grad_ref, grad_ref, out_recv).wait()


def per_device(projections, bias_terms, context_grad):
    proj = projections[0].transpose(0, 2, 1, 3)
    cot = context_grad.reshape(SEQ_LEN, 2 * HEAD_DIM)
    bf16, f32 = jnp.bfloat16, jnp.float32
    vmem = pl.BlockSpec(memory_space=pltpu.VMEM)
    anywhere = pl.BlockSpec(memory_space=pl.ANY)
    dma = pltpu.SemaphoreType.DMA
    context, grad, bias_grad = pl.pallas_call(
        kernel,
        out_shape=(
            jax.ShapeDtypeStruct((SEQ_LEN, 2 * HEAD_DIM), bf16),
            jax.ShapeDtypeStruct((2, 3, PIECE, WIDTH), bf16),
            jax.ShapeDtypeStruct((3, WIDTH), f32),
        ),
        in_specs=[vmem, vmem, anywhere],
        out_specs=(anywhere, anywhere, vmem),
        scratch_shapes=[
            pltpu.VMEM((2, 3, PIECE, WIDTH), bf16),
            pltpu.VMEM((2, 3, SEQ_LEN, HEAD_DIM), bf16),
            pltpu.VMEM((2, SEQ_LEN, HEAD_DIM), bf16),
            pltpu.VMEM((2, SEQ_LEN, HEAD_DIM), bf16),
            pltpu.VMEM((2, 3, SEQ_LEN, HEAD_DIM), bf16),
            pltpu.VMEM((SEQ_LEN, HEAD_DIM), f32),
            pltpu.VMEM((SEQ_LEN, HEAD_DIM), f32),
            pltpu.VMEM((HEAD_DIM, BLOCK), f32),
            pltpu.VMEM((HEAD_DIM, BLOCK), f32),
            pltpu.VMEM((SEQ_LEN, BLOCK), f32),
            pltpu.VMEM((SEQ_LEN, BLOCK), f32),
            pltpu.VMEM((HEAD_DIM, SEQ_LEN), bf16),
            pltpu.VMEM((HEAD_DIM, SEQ_LEN), bf16),
            pltpu.VMEM((2, 8, HEAD_DIM), f32),
            pltpu.VMEM((2, 8, HEAD_DIM), f32),
            pltpu.VMEM((16, 2, 8, HEAD_DIM), f32),
            pltpu.VMEM((16, 2, 8, HEAD_DIM), f32),
            dma((2, N_SHARD)), dma((2,)),
            dma((2,)), dma((2,)),
            dma((2, N_SHARD)), dma,
            dma((2,)), dma((2,)),
            dma((16,)), dma,
            dma((16,)), dma,
        ],
        compiler_params=pltpu.CompilerParams(
            collective_id=0, has_side_effects=True, vmem_limit_bytes=50 * 2**20
        ),
        cost_estimate=pl.CostEstimate(
            flops=8 * 10**9, bytes_accessed=10 * 2**20, transcendentals=5 * 10**6
        ),
    )(proj, bias_terms, cot)
    return (
        context.reshape(context_grad.shape),
        grad.transpose(0, 2, 1, 3)[None],
        bias_grad,
    )


def solution(mesh):
    placed = (
        P("section", "dp", "shard", None, None),
        P(),
        P("section", "dp", "shard", None, None, None),
    )
    return jax.shard_map(
        per_device,
        mesh=mesh,
        in_specs=placed,
        out_specs=(
            P("section", "dp", "shard", None, None, None),
            P("section", "dp", "shard", None, None),
            P(),
        ),
        check_vma=False,
    )
```

```python
import functools

import jax
import jax.numpy as jnp
from jax import lax
from jax.experimental import pallas as pl
from jax.experimental.pallas import tpu as pltpu
from jax.sharding import PartitionSpec as P

HEAD_DIM = 128
N_Z, N_Y, N_CORE = 4, 4, 2
N_SHARD = N_Z * N_Y * N_CORE
LINE = N_Y * N_CORE
PIECE = 64
SEQ_LEN = N_SHARD * PIECE
WIDTH = 4096
BLOCK = 512
FIRST_OUT = 24
CHUNK = 512
N_CHUNK = SEQ_LEN // CHUNK
N_BLOCK = SEQ_LEN // BLOCK
MESH = pl.DeviceIdType.MESH


def kernel(
    proj_ref, bias_hbm, cot_ref, context_ref, grad_ref, bias_grad_ref,
    biased, bias_ref, qkv, cot, ctx, grads, dk_acc, dv_acc, ctx_acc, dq_acc, score, dprob, k_t, v_t,
    part, total, stage1, stage2,
    in_send, in_recv, cot_send, cot_recv, out_send, out_recv, ctx_send, ctx_recv,
    s1_send, s1_recv, s2_send, s2_recv, load_sem, bias_sem,
):
    dp = lax.axis_index("dp")
    section = lax.axis_index("section")
    me = lax.axis_index("shard")
    z, inner = me // LINE, me % LINE
    y, core = inner // N_CORE, inner % N_CORE
    partner = (dp, 1 - section, (N_Z - 1 - z) * LINE + inner)
    scale = HEAD_DIM ** -0.5

    def peer(step):
        to_z = (z + step % N_Z) % N_Z
        rest = step // N_Z
        to_y = (y + rest // N_CORE) % N_Y
        to_core = (core + rest % N_CORE) % N_CORE
        return to_z * LINE + to_y * N_CORE + to_core

    def held_by(shard):
        home = (N_Z - 1 - shard // LINE) * LINE + shard % LINE
        return home // (N_SHARD // 2), (home % (N_SHARD // 2)) * 2

    def same_heads(step):
        return (dp + step // 4) % 4, (section + step // 2 % 2) % 2, ((z // 2 + step % 2) % 2) * 2 + z % 2

    def all_heads(step):
        to_z = z // 2 * 2 + (z % 2 + step // LINE) % 2
        to_y = (y + step % LINE // N_CORE) % N_Y
        to_core = (core + step % N_CORE) % N_CORE
        return to_z * LINE + to_y * N_CORE + to_core

    def load(n, kind):
        return pltpu.make_async_copy(proj_ref.at[n, kind], biased.at[n, kind], load_sem.at[n, kind])

    load_bias = pltpu.make_async_copy(bias_hbm, bias_ref, bias_sem)
    load_bias.start()
    for n in range(2):
        for kind in range(3):
            load(n, kind).start()

    barrier = pltpu.get_barrier_semaphore()

    def greet_section(step, carry):
        pl.semaphore_signal(barrier, inc=1, device_id=(dp, section, peer(step)), device_id_type=MESH)
        return carry

    lax.fori_loop(1, N_SHARD, greet_section, 0)
    pl.semaphore_signal(barrier, inc=1, device_id=partner, device_id_type=MESH)

    def greet_group(step, carry):
        to_dp, to_section, to_z = same_heads(step)
        pl.semaphore_signal(
            barrier, inc=1, device_id=(to_dp, to_section, to_z * LINE + inner), device_id_type=MESH
        )
        return carry

    lax.fori_loop(2, 16, greet_group, 0)

    load_bias.wait()
    for n in range(2):
        for kind in range(3):
            load(n, kind).wait()
            biased[n, kind] = (
                biased[n, kind].astype(jnp.float32) + bias_ref[kind:kind + 1, :]
            ).astype(jnp.bfloat16)

    pl.semaphore_wait(barrier, N_SHARD - 1 + 1 + 14)

    my_seq, my_head = held_by(me)
    my_rows = pl.ds(pl.multiple_of(me * PIECE, PIECE), PIECE)

    def columns(head):
        return pl.ds(pl.multiple_of(head * HEAD_DIM, HEAD_DIM), HEAD_DIM)

    def in_copy(step, h):
        to = peer(step)
        seq, head = held_by(to)
        return pltpu.make_async_remote_copy(
            src_ref=biased.at[seq, :, :, columns(head + h)],
            dst_ref=qkv.at[h, :, my_rows, :],
            send_sem=in_send.at[h, step],
            recv_sem=in_recv.at[h],
            device_id=(dp, section, to),
            device_id_type=MESH,
        )

    def out_copy(step, h):
        to = peer(step)
        rows = pl.ds(pl.multiple_of(to * PIECE, PIECE), PIECE)
        return pltpu.make_async_remote_copy(
            src_ref=grads.at[h, :, rows, :],
            dst_ref=grad_ref.at[my_seq, :, :, columns(my_head + h)],
            send_sem=out_send.at[h, step],
            recv_sem=out_recv,
            device_id=(dp, section, to),
            device_id_type=MESH,
        )

    def chunk_rows(chunk):
        return pl.ds(pl.multiple_of(chunk * CHUNK, CHUNK), CHUNK)

    def cot_copy(h, chunk):
        return pltpu.make_async_remote_copy(
            src_ref=cot_ref.at[chunk_rows(chunk), columns(h)],
            dst_ref=cot.at[h, chunk_rows(chunk), :],
            send_sem=cot_send.at[h, chunk],
            recv_sem=cot_recv.at[h],
            device_id=partner,
            device_id_type=MESH,
        )

    def ctx_copy(h, chunk):
        return pltpu.make_async_remote_copy(
            src_ref=ctx.at[h, chunk_rows(chunk), :],
            dst_ref=context_ref.at[chunk_rows(chunk), columns(h)],
            send_sem=ctx_send.at[h, chunk],
            recv_sem=ctx_recv,
            device_id=partner,
            device_id_type=MESH,
        )

    def start_cot(h):
        def body(chunk, carry):
            cot_copy(h, chunk).start()
            return carry
        lax.fori_loop(0, N_CHUNK, body, 0)

    def start_in(step, carry):
        in_copy(step, 0).start()
        return carry

    for h in range(2):
        pltpu.make_async_copy(
            biased.at[my_seq, :, :, columns(my_head + h)], qkv.at[h, :, my_rows, :], in_recv.at[h]
        ).start()
    start_cot(0)
    lax.fori_loop(1, N_SHARD, start_in, 0)

    def follow_in(step, carry):
        in_copy(step, 0).wait_send()
        in_copy(step, 1).start()
        return carry

    lax.fori_loop(1, N_SHARD, follow_in, 0)
    start_cot(1)

    part[...] = jnp.zeros_like(part)

    def rows_of(block):
        return pl.ds(pl.multiple_of(block * BLOCK, BLOCK), BLOCK)

    group = (dp * 2 + section) * 2 + z // 2
    pair = my_head // 2

    def s1_copy(step):
        to_dp, to_section, to_z = same_heads(step)
        return pltpu.make_async_remote_copy(
            src_ref=part, dst_ref=stage1.at[group], send_sem=s1_send.at[step], recv_sem=s1_recv,
            device_id=(to_dp, to_section, to_z * LINE + inner), device_id_type=MESH,
        )

    def s2_copy(step):
        return pltpu.make_async_remote_copy(
            src_ref=total, dst_ref=stage2.at[pair], send_sem=s2_send.at[step], recv_sem=s2_recv,
            device_id=(dp, section, all_heads(step)), device_id_type=MESH,
        )

    def run(make, method):
        def body(step, carry):
            getattr(make(step), method)()
            return carry
        lax.fori_loop(1, 16, body, 0)

    def head_step(h, carry):
        pltpu.make_async_copy(qkv.at[h], qkv.at[h], in_recv.at[h]).wait()

        def turn(c, carry):
            k_t[:, rows_of(c)] = qkv[h, 1, rows_of(c), :].T
            v_t[:, rows_of(c)] = qkv[h, 2, rows_of(c), :].T
            return carry

        lax.fori_loop(0, N_BLOCK, turn, 0)
        dk_acc[...] = jnp.zeros_like(dk_acc)
        dv_acc[...] = jnp.zeros_like(dv_acc)
        pltpu.make_async_copy(cot.at[h], cot.at[h], cot_recv.at[h]).wait()

        def query_block(b, carry):
            query = qkv[h, 0, rows_of(b), :]
            grad_out = cot[h, rows_of(b), :]
            ctx_acc[...] = jnp.zeros_like(ctx_acc)
            dq_acc[...] = jnp.zeros_like(dq_acc)

            def scores_of(c):
                return lax.dot_general(
                    qkv[h, 1, rows_of(c), :], query, (((1,), (1,)), ((), ())),
                    preferred_element_type=jnp.float32,
                ) * scale

            def first(c, top):
                s = scores_of(c)
                score[rows_of(c), :] = s
                return jnp.maximum(top, jnp.max(s, axis=0, keepdims=True))

            top = lax.fori_loop(0, b, first, jnp.full((1, BLOCK), -jnp.inf, jnp.float32))
            s = scores_of(b)
            key_id = lax.broadcasted_iota(jnp.int32, s.shape, 0)
            query_id = lax.broadcasted_iota(jnp.int32, s.shape, 1)
            s = jnp.where(key_id <= query_id, s, -jnp.inf)
            score[rows_of(b), :] = s
            top = jnp.maximum(top, jnp.max(s, axis=0, keepdims=True))

            def second(c, denom):
                e = jnp.exp(score[rows_of(c), :] - top)
                score[rows_of(c), :] = e
                return denom + jnp.sum(e, axis=0, keepdims=True)

            denom = lax.fori_loop(0, b + 1, second, jnp.zeros((1, BLOCK), jnp.float32))
            inverse = 1.0 / denom

            def third(c, delta):
                probability = score[rows_of(c), :] * inverse
                weights = probability.astype(jnp.bfloat16)
                ctx_acc[...] += jnp.dot(v_t[:, rows_of(c)], weights, preferred_element_type=jnp.float32)
                dv_acc[rows_of(c), :] += jnp.dot(weights, grad_out, preferred_element_type=jnp.float32)
                grad_prob = lax.dot_general(
                    qkv[h, 2, rows_of(c), :], grad_out, (((1,), (1,)), ((), ())),
                    preferred_element_type=jnp.float32,
                )
                dprob[rows_of(c), :] = grad_prob
                return delta + jnp.sum(probability * grad_prob, axis=0, keepdims=True)

            delta = lax.fori_loop(0, b + 1, third, jnp.zeros((1, BLOCK), jnp.float32))

            def fourth(c, carry):
                probability = score[rows_of(c), :] * inverse
                grad_score = (probability * (dprob[rows_of(c), :] - delta) * scale).astype(jnp.bfloat16)
                dq_acc[...] += jnp.dot(k_t[:, rows_of(c)], grad_score, preferred_element_type=jnp.float32)
                dk_acc[rows_of(c), :] += jnp.dot(grad_score, query, preferred_element_type=jnp.float32)
                return carry

            lax.fori_loop(0, b + 1, fourth, 0)
            ctx[h, rows_of(b), :] = ctx_acc[...].T.astype(jnp.bfloat16)
            grads[h, 0, rows_of(b), :] = dq_acc[...].T.astype(jnp.bfloat16)
            for part_id in range(BLOCK // CHUNK):
                ctx_copy(h, b * (BLOCK // CHUNK) + part_id).start()
            return carry

        lax.fori_loop(0, N_BLOCK, query_block, 0)

        def finish(c, carry):
            dk = dk_acc[rows_of(c), :].astype(jnp.bfloat16)
            dv = dv_acc[rows_of(c), :].astype(jnp.bfloat16)
            grads[h, 1, rows_of(c), :] = dk
            grads[h, 2, rows_of(c), :] = dv
            dq = grads[h, 0, rows_of(c), :]
            return tuple(
                acc + jnp.sum(x.astype(jnp.float32), axis=0, keepdims=True)
                for acc, x in zip(carry, (dq, dk, dv))
            )

        sums = lax.fori_loop(0, N_BLOCK, finish, (jnp.zeros((1, HEAD_DIM), jnp.float32),) * 3)
        for kind in range(3):
            part[pl.ds(h * 3 + kind, 1), :] = sums[kind]

        @pl.when(h == 1)
        def _():
            pltpu.make_async_copy(part, stage1.at[group], s1_recv).start()
            run(s1_copy, "start")

        own = pltpu.make_async_copy(
            grads.at[h, :, my_rows, :], grad_ref.at[my_seq, :, :, columns(my_head + h)], out_recv
        )
        own.start()

        def start_out(step, carry):
            out_copy(step, h).start()
            return carry

        lax.fori_loop(1, FIRST_OUT, start_out, 0)

        @pl.when(h == 1)
        def _():
            pltpu.make_async_copy(stage1, stage1, s1_recv).wait()
            total[...] = jnp.sum(stage1[...], axis=0)
            pltpu.make_async_copy(total, stage2.at[pair], s2_recv).start()
            run(s2_copy, "start")

        lax.fori_loop(FIRST_OUT, N_SHARD, start_out, 0)
        return carry

    lax.fori_loop(0, 2, head_step, 0)

    pltpu.make_async_copy(stage2, stage2, s2_recv).wait()
    for p in range(16):
        for h in range(2):
            first_column = (p * 2 + h) * HEAD_DIM
            bias_grad_ref[:, first_column:first_column + HEAD_DIM] = stage2[p, h * 3:h * 3 + 3, :]
    run(s1_copy, "wait_send")
    run(s2_copy, "wait_send")

    def drain(step, carry):
        in_copy(step, 1).wait_send()
        out_copy(step, 0).wait_send()
        out_copy(step, 1).wait_send()
        return carry

    lax.fori_loop(1, N_SHARD, drain, 0)

    def drain_chunks(chunk, carry):
        for h in range(2):
            cot_copy(h, chunk).wait_send()
            ctx_copy(h, chunk).wait_send()
        return carry

    lax.fori_loop(0, N_CHUNK, drain_chunks, 0)
    pltpu.make_async_copy(context_ref, context_ref, ctx_recv).wait()
    pltpu.make_async_copy(grad_ref, grad_ref, out_recv).wait()


def per_device(projections, bias_terms, context_grad):
    proj = projections[0].transpose(0, 2, 1, 3)
    cot = context_grad.reshape(SEQ_LEN, 2 * HEAD_DIM)
    bf16, f32 = jnp.bfloat16, jnp.float32
    vmem = pl.BlockSpec(memory_space=pltpu.VMEM)
    anywhere = pl.BlockSpec(memory_space=pl.ANY)
    hbm = pl.BlockSpec(memory_space=pltpu.HBM)
    dma = pltpu.SemaphoreType.DMA
    context, grad, bias_grad = pl.pallas_call(
        kernel,
        out_shape=(
            jax.ShapeDtypeStruct((SEQ_LEN, 2 * HEAD_DIM), bf16),
            jax.ShapeDtypeStruct((2, 3, PIECE, WIDTH), bf16),
            jax.ShapeDtypeStruct((3, WIDTH), f32),
        ),
        in_specs=[hbm, hbm, hbm],
        out_specs=(anywhere, anywhere, vmem),
        scratch_shapes=[
            pltpu.VMEM((2, 3, PIECE, WIDTH), bf16),
            pltpu.VMEM((3, WIDTH), f32),
            pltpu.VMEM((2, 3, SEQ_LEN, HEAD_DIM), bf16),
            pltpu.VMEM((2, SEQ_LEN, HEAD_DIM), bf16),
            pltpu.VMEM((2, SEQ_LEN, HEAD_DIM), bf16),
            pltpu.VMEM((2, 3, SEQ_LEN, HEAD_DIM), bf16),
            pltpu.VMEM((SEQ_LEN, HEAD_DIM), f32),
            pltpu.VMEM((SEQ_LEN, HEAD_DIM), f32),
            pltpu.VMEM((HEAD_DIM, BLOCK), f32),
            pltpu.VMEM((HEAD_DIM, BLOCK), f32),
            pltpu.VMEM((SEQ_LEN, BLOCK), f32),
            pltpu.VMEM((SEQ_LEN, BLOCK), f32),
            pltpu.VMEM((HEAD_DIM, SEQ_LEN), bf16),
            pltpu.VMEM((HEAD_DIM, SEQ_LEN), bf16),
            pltpu.VMEM((8, HEAD_DIM), f32),
            pltpu.VMEM((8, HEAD_DIM), f32),
            pltpu.VMEM((16, 8, HEAD_DIM), f32),
            pltpu.VMEM((16, 8, HEAD_DIM), f32),
            dma((2, N_SHARD)), dma((2,)),
            dma((2, N_CHUNK)), dma((2,)),
            dma((2, N_SHARD)), dma,
            dma((2, N_CHUNK)), dma,
            dma((16,)), dma,
            dma((16,)), dma,
            dma((2, 3)), dma,
        ],
        compiler_params=pltpu.CompilerParams(
            collective_id=0, has_side_effects=True, vmem_limit_bytes=36 * 2**20
        ),
        cost_estimate=pl.CostEstimate(
            flops=8 * 10**9, bytes_accessed=10 * 2**20, transcendentals=5 * 10**6
        ),
    )(*(pltpu.with_memory_space_constraint(x, pltpu.HBM) for x in (proj, bias_terms, cot)))
    return (
        context.reshape(context_grad.shape),
        grad.transpose(0, 2, 1, 3)[None],
        bias_grad,
    )


def solution(mesh):
    placed = (
        P("section", "dp", "shard", None, None),
        P(),
        P("section", "dp", "shard", None, None, None),
    )
    return jax.shard_map(
        per_device,
        mesh=mesh,
        in_specs=placed,
        out_specs=(
            P("section", "dp", "shard", None, None, None),
            P("section", "dp", "shard", None, None),
            P(),
        ),
        check_vma=False,
    )
```

```python
import functools

import jax
import jax.numpy as jnp
from jax import lax
from jax.experimental import pallas as pl
from jax.experimental.pallas import tpu as pltpu
from jax.sharding import PartitionSpec as P

HEAD_DIM = 128
N_Z, N_Y, N_CORE = 4, 4, 2
N_SHARD = N_Z * N_Y * N_CORE
LINE = N_Y * N_CORE
PIECE = 64
SEQ_LEN = N_SHARD * PIECE
WIDTH = 4096
BLOCK = 512
FIRST_OUT = 28
CHUNK = 512
N_CHUNK = SEQ_LEN // CHUNK
N_BLOCK = SEQ_LEN // BLOCK
MESH = pl.DeviceIdType.MESH


def kernel(
    proj_ref, bias_hbm, cot_ref, context_ref, grad_ref, bias_grad_ref,
    biased, bias_ref, qkv, cot, ctx, grads, dk_acc, dv_acc, ctx_acc, dq_acc, score, dprob, k_t, v_t,
    part, total, stage1, stage2,
    in_send, in_recv, cot_send, cot_recv, out_send, out_recv, ctx_send, ctx_recv,
    s1_send, s1_recv, s2_send, s2_recv, load_sem, bias_sem, ready,
):
    dp = lax.axis_index("dp")
    section = lax.axis_index("section")
    me = lax.axis_index("shard")
    z, inner = lax.div(me, LINE), lax.rem(me, LINE)
    y, core = lax.div(inner, N_CORE), lax.rem(inner, N_CORE)
    partner = (dp, 1 - section, (N_Z - 1 - z) * LINE + inner)
    scale = HEAD_DIM ** -0.5

    def split(value, by):
        if isinstance(value, int):
            return value // by, value % by
        return lax.div(value, by), lax.rem(value, by)

    def peer(step):
        rest, step_z = split(step, N_Z)
        step_y, step_core = split(rest, N_CORE)
        to_z = lax.rem(z + step_z, N_Z)
        to_y = lax.rem(y + step_y, N_Y)
        to_core = lax.rem(core + step_core, N_CORE)
        return to_z * LINE + to_y * N_CORE + to_core

    def held_by(shard):
        shard_z, shard_inner = split(shard, LINE)
        home_z = N_Z - 1 - shard_z
        seq, odd = split(home_z, 2)
        return seq, (odd * LINE + shard_inner) * 2

    z_pair, z_odd = split(z, 2)

    def same_heads(step):
        rest, step_pair = split(step, 2)
        step_dp, step_section = split(rest, 2)
        to_pair = lax.rem(z_pair + step_pair, 2)
        return lax.rem(dp + step_dp, 4), lax.rem(section + step_section, 2), to_pair * 2 + z_odd

    def all_heads(step):
        step_odd, rest = split(step, LINE)
        step_y, step_core = split(rest, N_CORE)
        to_z = z_pair * 2 + lax.rem(z_odd + step_odd, 2)
        to_y = lax.rem(y + step_y, N_Y)
        to_core = lax.rem(core + step_core, N_CORE)
        return to_z * LINE + to_y * N_CORE + to_core

    barrier = pltpu.get_barrier_semaphore()

    def tell(sem, device):
        pl.semaphore_signal(sem, inc=1, device_id=device, device_id_type=MESH)

    def group_device(step):
        to_dp, to_section, to_z = same_heads(step)
        return to_dp, to_section, to_z * LINE + inner

    near = [step for step in range(2, 16) if step // 2 % 2 == 0]
    far = [step for step in range(2, 16) if step // 2 % 2 == 1]

    for step in range(1, N_SHARD):
        tell(barrier, (dp, section, peer(step)))
    for step in near:
        tell(barrier, group_device(step))

    @pl.when(section == 0)
    def _():
        tell(barrier, partner)
        for step in far:
            tell(barrier, group_device(step))

    def load(n, kind):
        return pltpu.make_async_copy(proj_ref.at[n, kind], biased.at[n, kind], load_sem.at[n, kind])

    load_bias = pltpu.make_async_copy(bias_hbm, bias_ref, bias_sem)
    load_bias.start()
    for n in range(2):
        for kind in range(3):
            load(n, kind).start()

    load_bias.wait()
    for n in range(2):
        for kind in range(3):
            load(n, kind).wait()
            biased[n, kind] = (
                biased[n, kind].astype(jnp.float32) + bias_ref[kind:kind + 1, :]
            ).astype(jnp.bfloat16)

    @pl.when(section == 0)
    def _():
        pl.semaphore_wait(barrier, N_SHARD - 1 + len(near))

    @pl.when(section == 1)
    def _():
        pl.semaphore_wait(barrier, N_SHARD - 1 + len(near) + 1 + len(far))
        tell(ready, partner)
        for step in far:
            tell(ready, group_device(step))

    my_seq, my_head = held_by(me)
    my_rows = pl.ds(pl.multiple_of(me * PIECE, PIECE), PIECE)

    def columns(head):
        return pl.ds(pl.multiple_of(head * HEAD_DIM, HEAD_DIM), HEAD_DIM)

    def in_copy(step, h):
        to = peer(step)
        seq, head = held_by(to)
        return pltpu.make_async_remote_copy(
            src_ref=biased.at[seq, :, :, columns(head + h)],
            dst_ref=qkv.at[h, :, my_rows, :],
            send_sem=in_send.at[h, step],
            recv_sem=in_recv.at[h],
            device_id=(dp, section, to),
            device_id_type=MESH,
        )

    def out_copy(step, h):
        to = peer(step)
        rows = pl.ds(pl.multiple_of(to * PIECE, PIECE), PIECE)
        return pltpu.make_async_remote_copy(
            src_ref=grads.at[h, :, rows, :],
            dst_ref=grad_ref.at[my_seq, :, :, columns(my_head + h)],
            send_sem=out_send.at[h, step],
            recv_sem=out_recv,
            device_id=(dp, section, to),
            device_id_type=MESH,
        )

    def chunk_rows(chunk):
        return pl.ds(pl.multiple_of(chunk * CHUNK, CHUNK), CHUNK)

    def cot_copy(h, chunk):
        return pltpu.make_async_remote_copy(
            src_ref=cot_ref.at[chunk_rows(chunk), columns(h)],
            dst_ref=cot.at[h, chunk_rows(chunk), :],
            send_sem=cot_send.at[h, chunk],
            recv_sem=cot_recv.at[h],
            device_id=partner,
            device_id_type=MESH,
        )

    def ctx_copy(h, chunk):
        return pltpu.make_async_remote_copy(
            src_ref=ctx.at[h, chunk_rows(chunk), :],
            dst_ref=context_ref.at[chunk_rows(chunk), columns(h)],
            send_sem=ctx_send.at[h, chunk],
            recv_sem=ctx_recv,
            device_id=partner,
            device_id_type=MESH,
        )

    def start_cot(h):
        def body(chunk, carry):
            cot_copy(h, chunk).start()
            return carry
        lax.fori_loop(0, N_CHUNK, body, 0)

    def start_in(step, carry):
        in_copy(step, 0).start()
        return carry

    for h in range(2):
        pltpu.make_async_copy(
            biased.at[my_seq, :, :, columns(my_head + h)], qkv.at[h, :, my_rows, :], in_recv.at[h]
        ).start()
    lax.fori_loop(1, N_SHARD, start_in, 0)

    @pl.when(section == 0)
    def _():
        pl.semaphore_wait(ready, 1 + len(far))

    start_cot(0)

    def follow_in(step, carry):
        in_copy(step, 0).wait_send()
        in_copy(step, 1).start()
        return carry

    lax.fori_loop(1, N_SHARD, follow_in, 0)
    start_cot(1)

    part[...] = jnp.zeros_like(part)

    def rows_of(block):
        return pl.ds(pl.multiple_of(block * BLOCK, BLOCK), BLOCK)

    group = (dp * 2 + section) * 2 + z_pair
    pair = lax.div(my_head, 2)

    def s1_copy(step):
        to_dp, to_section, to_z = same_heads(step)
        return pltpu.make_async_remote_copy(
            src_ref=part, dst_ref=stage1.at[group], send_sem=s1_send.at[step], recv_sem=s1_recv,
            device_id=(to_dp, to_section, to_z * LINE + inner), device_id_type=MESH,
        )

    def s2_copy(step):
        return pltpu.make_async_remote_copy(
            src_ref=total, dst_ref=stage2.at[pair], send_sem=s2_send.at[step], recv_sem=s2_recv,
            device_id=(dp, section, all_heads(step)), device_id_type=MESH,
        )

    def run(make, method):
        def body(step, carry):
            getattr(make(step), method)()
            return carry
        lax.fori_loop(1, 16, body, 0)

    def head_step(h, carry):
        pltpu.make_async_copy(qkv.at[h], qkv.at[h], in_recv.at[h]).wait()

        def turn(c, carry):
            k_t[:, rows_of(c)] = qkv[h, 1, rows_of(c), :].T
            v_t[:, rows_of(c)] = qkv[h, 2, rows_of(c), :].T
            return carry

        lax.fori_loop(0, N_BLOCK, turn, 0)
        dk_acc[...] = jnp.zeros_like(dk_acc)
        dv_acc[...] = jnp.zeros_like(dv_acc)
        pltpu.make_async_copy(cot.at[h], cot.at[h], cot_recv.at[h]).wait()

        def query_block(b, carry):
            query = qkv[h, 0, rows_of(b), :]
            grad_out = cot[h, rows_of(b), :]
            ctx_acc[...] = jnp.zeros_like(ctx_acc)
            dq_acc[...] = jnp.zeros_like(dq_acc)

            def scores_of(c):
                return lax.dot_general(
                    qkv[h, 1, rows_of(c), :], query, (((1,), (1,)), ((), ())),
                    preferred_element_type=jnp.float32,
                ) * scale

            def first(c, top):
                s = scores_of(c)
                score[rows_of(c), :] = s
                return jnp.maximum(top, jnp.max(s, axis=0, keepdims=True))

            top = lax.fori_loop(0, b, first, jnp.full((1, BLOCK), -jnp.inf, jnp.float32))
            s = scores_of(b)
            key_id = lax.broadcasted_iota(jnp.int32, s.shape, 0)
            query_id = lax.broadcasted_iota(jnp.int32, s.shape, 1)
            s = jnp.where(key_id <= query_id, s, -jnp.inf)
            score[rows_of(b), :] = s
            top = jnp.maximum(top, jnp.max(s, axis=0, keepdims=True))

            def second(c, denom):
                e = jnp.exp(score[rows_of(c), :] - top)
                score[rows_of(c), :] = e
                return denom + jnp.sum(e, axis=0, keepdims=True)

            denom = lax.fori_loop(0, b + 1, second, jnp.zeros((1, BLOCK), jnp.float32))
            inverse = 1.0 / denom

            def third(c, delta):
                probability = score[rows_of(c), :] * inverse
                weights = probability.astype(jnp.bfloat16)
                ctx_acc[...] += jnp.dot(v_t[:, rows_of(c)], weights, preferred_element_type=jnp.float32)
                dv_acc[rows_of(c), :] += jnp.dot(weights, grad_out, preferred_element_type=jnp.float32)
                grad_prob = lax.dot_general(
                    qkv[h, 2, rows_of(c), :], grad_out, (((1,), (1,)), ((), ())),
                    preferred_element_type=jnp.float32,
                )
                dprob[rows_of(c), :] = grad_prob
                return delta + jnp.sum(probability * grad_prob, axis=0, keepdims=True)

            delta = lax.fori_loop(0, b + 1, third, jnp.zeros((1, BLOCK), jnp.float32))

            def fourth(c, carry):
                probability = score[rows_of(c), :] * inverse
                grad_score = (probability * (dprob[rows_of(c), :] - delta) * scale).astype(jnp.bfloat16)
                dq_acc[...] += jnp.dot(k_t[:, rows_of(c)], grad_score, preferred_element_type=jnp.float32)
                dk_acc[rows_of(c), :] += jnp.dot(grad_score, query, preferred_element_type=jnp.float32)
                return carry

            lax.fori_loop(0, b + 1, fourth, 0)
            ctx[h, rows_of(b), :] = ctx_acc[...].T.astype(jnp.bfloat16)
            grads[h, 0, rows_of(b), :] = dq_acc[...].T.astype(jnp.bfloat16)
            for part_id in range(BLOCK // CHUNK):
                ctx_copy(h, b * (BLOCK // CHUNK) + part_id).start()
            return carry

        lax.fori_loop(0, N_BLOCK, query_block, 0)

        def finish(c, carry):
            dk = dk_acc[rows_of(c), :].astype(jnp.bfloat16)
            dv = dv_acc[rows_of(c), :].astype(jnp.bfloat16)
            grads[h, 1, rows_of(c), :] = dk
            grads[h, 2, rows_of(c), :] = dv
            dq = grads[h, 0, rows_of(c), :]
            return tuple(
                acc + jnp.sum(x.astype(jnp.float32), axis=0, keepdims=True)
                for acc, x in zip(carry, (dq, dk, dv))
            )

        sums = lax.fori_loop(0, N_BLOCK, finish, (jnp.zeros((1, HEAD_DIM), jnp.float32),) * 3)
        for kind in range(3):
            part[pl.ds(h * 3 + kind, 1), :] = sums[kind]

        @pl.when(h == 1)
        def _():
            pltpu.make_async_copy(part, stage1.at[group], s1_recv).start()
            run(s1_copy, "start")

        own = pltpu.make_async_copy(
            grads.at[h, :, my_rows, :], grad_ref.at[my_seq, :, :, columns(my_head + h)], out_recv
        )
        own.start()

        def start_out(step, carry):
            out_copy(step, h).start()
            return carry

        lax.fori_loop(1, FIRST_OUT, start_out, 0)

        @pl.when(h == 1)
        def _():
            pltpu.make_async_copy(stage1, stage1, s1_recv).wait()
            total[...] = jnp.sum(stage1[...], axis=0)
            pltpu.make_async_copy(total, stage2.at[pair], s2_recv).start()
            run(s2_copy, "start")

        lax.fori_loop(FIRST_OUT, N_SHARD, start_out, 0)
        return carry

    lax.fori_loop(0, 2, head_step, 0)

    pltpu.make_async_copy(stage2, stage2, s2_recv).wait()
    for p in range(16):
        for h in range(2):
            first_column = (p * 2 + h) * HEAD_DIM
            bias_grad_ref[:, first_column:first_column + HEAD_DIM] = stage2[p, h * 3:h * 3 + 3, :]
    run(s1_copy, "wait_send")
    run(s2_copy, "wait_send")

    def drain(step, carry):
        in_copy(step, 1).wait_send()
        out_copy(step, 0).wait_send()
        out_copy(step, 1).wait_send()
        return carry

    lax.fori_loop(1, N_SHARD, drain, 0)

    def drain_chunks(chunk, carry):
        for h in range(2):
            cot_copy(h, chunk).wait_send()
            ctx_copy(h, chunk).wait_send()
        return carry

    lax.fori_loop(0, N_CHUNK, drain_chunks, 0)
    pltpu.make_async_copy(context_ref, context_ref, ctx_recv).wait()
    pltpu.make_async_copy(grad_ref, grad_ref, out_recv).wait()


def per_device(projections, bias_terms, context_grad):
    proj = projections[0].transpose(0, 2, 1, 3)
    cot = context_grad.reshape(SEQ_LEN, 2 * HEAD_DIM)
    bf16, f32 = jnp.bfloat16, jnp.float32
    vmem = pl.BlockSpec(memory_space=pltpu.VMEM)
    anywhere = pl.BlockSpec(memory_space=pl.ANY)
    hbm = pl.BlockSpec(memory_space=pltpu.HBM)
    dma = pltpu.SemaphoreType.DMA
    context, grad, bias_grad = pl.pallas_call(
        kernel,
        out_shape=(
            jax.ShapeDtypeStruct((SEQ_LEN, 2 * HEAD_DIM), bf16),
            jax.ShapeDtypeStruct((2, 3, PIECE, WIDTH), bf16),
            jax.ShapeDtypeStruct((3, WIDTH), f32),
        ),
        in_specs=[hbm, hbm, hbm],
        out_specs=(anywhere, anywhere, vmem),
        scratch_shapes=[
            pltpu.VMEM((2, 3, PIECE, WIDTH), bf16),
            pltpu.VMEM((3, WIDTH), f32),
            pltpu.VMEM((2, 3, SEQ_LEN, HEAD_DIM), bf16),
            pltpu.VMEM((2, SEQ_LEN, HEAD_DIM), bf16),
            pltpu.VMEM((2, SEQ_LEN, HEAD_DIM), bf16),
            pltpu.VMEM((2, 3, SEQ_LEN, HEAD_DIM), bf16),
            pltpu.VMEM((SEQ_LEN, HEAD_DIM), f32),
            pltpu.VMEM((SEQ_LEN, HEAD_DIM), f32),
            pltpu.VMEM((HEAD_DIM, BLOCK), f32),
            pltpu.VMEM((HEAD_DIM, BLOCK), f32),
            pltpu.VMEM((SEQ_LEN, BLOCK), f32),
            pltpu.VMEM((SEQ_LEN, BLOCK), f32),
            pltpu.VMEM((HEAD_DIM, SEQ_LEN), bf16),
            pltpu.VMEM((HEAD_DIM, SEQ_LEN), bf16),
            pltpu.VMEM((8, HEAD_DIM), f32),
            pltpu.VMEM((8, HEAD_DIM), f32),
            pltpu.VMEM((16, 8, HEAD_DIM), f32),
            pltpu.VMEM((16, 8, HEAD_DIM), f32),
            dma((2, N_SHARD)), dma((2,)),
            dma((2, N_CHUNK)), dma((2,)),
            dma((2, N_SHARD)), dma,
            dma((2, N_CHUNK)), dma,
            dma((16,)), dma,
            dma((16,)), dma,
            dma((2, 3)), dma,
            pltpu.SemaphoreType.REGULAR,
        ],
        compiler_params=pltpu.CompilerParams(
            collective_id=0, has_side_effects=True, vmem_limit_bytes=36 * 2**20
        ),
        cost_estimate=pl.CostEstimate(
            flops=8 * 10**9, bytes_accessed=10 * 2**20, transcendentals=5 * 10**6
        ),
    )(*(pltpu.with_memory_space_constraint(x, pltpu.HBM) for x in (proj, bias_terms, cot)))
    return (
        context.reshape(context_grad.shape),
        grad.transpose(0, 2, 1, 3)[None],
        bias_grad,
    )


def solution(mesh):
    placed = (
        P("section", "dp", "shard", None, None),
        P(),
        P("section", "dp", "shard", None, None, None),
    )
    return jax.shard_map(
        per_device,
        mesh=mesh,
        in_specs=placed,
        out_specs=(
            P("section", "dp", "shard", None, None, None),
            P("section", "dp", "shard", None, None),
            P(),
        ),
        check_vma=False,
    )
```

```python
import functools

import jax
import jax.numpy as jnp
from jax import lax
from jax.experimental import pallas as pl
from jax.experimental.pallas import tpu as pltpu
from jax.sharding import PartitionSpec as P

HEAD_DIM = 128
N_DP, N_Z, N_Y, N_CORE = 4, 4, 4, 2
N_SHARD = N_Z * N_Y * N_CORE
LINE = N_Y * N_CORE
PIECE = 64
SEQ_LEN = N_SHARD * PIECE
WIDTH = 4096
BLOCK = 512
SECOND_STAGE = 16
THIRD_STAGE = 26
CHUNK = 512
N_CHUNK = SEQ_LEN // CHUNK
N_BLOCK = SEQ_LEN // BLOCK
MESH = pl.DeviceIdType.MESH


def kernel(
    proj_ref, bias_hbm, cot_ref, context_ref, grad_ref, bias_grad_ref,
    biased, bias_ref, qkv, cot, ctx, grads, dk_acc, dv_acc, ctx_acc, dq_acc, score, dprob, k_t, v_t,
    part, total, pairs, stage1, stage2, stage3,
    in_send, in_recv, cot_send, cot_recv, out_send, out_recv, ctx_send, ctx_recv,
    s1_send, s1_recv, s2_send, s2_recv, s3_send, s3_recv, load_sem, bias_sem, ready,
):
    dp = lax.axis_index("dp")
    section = lax.axis_index("section")
    me = lax.axis_index("shard")
    z, inner = lax.div(me, LINE), lax.rem(me, LINE)
    y, core = lax.div(inner, N_CORE), lax.rem(inner, N_CORE)
    partner = (dp, 1 - section, (N_Z - 1 - z) * LINE + inner)
    scale = HEAD_DIM ** -0.5

    def split(value, by):
        if isinstance(value, int):
            return value // by, value % by
        return lax.div(value, by), lax.rem(value, by)

    def peer(step):
        rest, step_z = split(N_SHARD - step, N_Z)
        step_y, step_core = split(rest, N_CORE)
        to_z = lax.rem(z + step_z, N_Z)
        to_y = lax.rem(y + step_y, N_Y)
        to_core = lax.rem(core + step_core, N_CORE)
        return to_z * LINE + to_y * N_CORE + to_core

    def held_by(shard):
        shard_z, shard_inner = split(shard, LINE)
        home_z = N_Z - 1 - shard_z
        seq, odd = split(home_z, 2)
        return seq, (odd * LINE + shard_inner) * 2

    ring = section * N_Z + z

    def dp_device(step):
        return lax.rem(dp + step, N_DP), section, me

    def ring_device(step):
        to_section, to_z = split(lax.rem(ring + step, 2 * N_Z), N_Z)
        return dp, to_section, to_z * LINE + inner

    def plane_device(step):
        step_y, step_core = split(step, N_CORE)
        to_y = lax.rem(y + step_y, N_Y)
        to_core = lax.rem(core + step_core, N_CORE)
        return dp, section, z * LINE + to_y * N_CORE + to_core

    barrier = pltpu.get_barrier_semaphore()

    def tell(sem, device):
        pl.semaphore_signal(sem, inc=1, device_id=device, device_id_type=MESH)

    def other_section(h):
        return dp, 1 - section, h * LINE + inner

    for step in range(1, N_SHARD):
        tell(barrier, (dp, section, peer(step)))
    for step in range(1, N_DP):
        tell(barrier, dp_device(step))

    @pl.when(section == 0)
    def _():
        for far_z in range(N_Z):
            tell(barrier, other_section(far_z))

    def load(n, kind):
        return pltpu.make_async_copy(proj_ref.at[n, kind], biased.at[n, kind], load_sem.at[n, kind])

    load_bias = pltpu.make_async_copy(bias_hbm, bias_ref, bias_sem)
    load_bias.start()
    for n in range(2):
        for kind in range(3):
            load(n, kind).start()

    load_bias.wait()
    for n in range(2):
        for kind in range(3):
            load(n, kind).wait()
            biased[n, kind] = (
                biased[n, kind].astype(jnp.float32) + bias_ref[kind:kind + 1, :]
            ).astype(jnp.bfloat16)

    @pl.when(section == 0)
    def _():
        pl.semaphore_wait(barrier, N_SHARD - 1 + N_DP - 1)

    @pl.when(section == 1)
    def _():
        pl.semaphore_wait(barrier, N_SHARD - 1 + N_DP - 1 + N_Z)
        for far_z in range(N_Z):
            tell(ready, other_section(far_z))

    my_seq, my_head = held_by(me)
    my_rows = pl.ds(pl.multiple_of(me * PIECE, PIECE), PIECE)

    def columns(head):
        return pl.ds(pl.multiple_of(head * HEAD_DIM, HEAD_DIM), HEAD_DIM)

    def in_copy(step, h):
        to = peer(step)
        seq, head = held_by(to)
        return pltpu.make_async_remote_copy(
            src_ref=biased.at[seq, :, :, columns(head + h)],
            dst_ref=qkv.at[h, :, my_rows, :],
            send_sem=in_send.at[h, step],
            recv_sem=in_recv.at[h],
            device_id=(dp, section, to),
            device_id_type=MESH,
        )

    def out_copy(step, h):
        to = peer(step)
        rows = pl.ds(pl.multiple_of(to * PIECE, PIECE), PIECE)
        return pltpu.make_async_remote_copy(
            src_ref=grads.at[h, :, rows, :],
            dst_ref=grad_ref.at[my_seq, :, :, columns(my_head + h)],
            send_sem=out_send.at[h, step],
            recv_sem=out_recv,
            device_id=(dp, section, to),
            device_id_type=MESH,
        )

    def chunk_rows(chunk):
        return pl.ds(pl.multiple_of(chunk * CHUNK, CHUNK), CHUNK)

    def cot_copy(h, chunk):
        return pltpu.make_async_remote_copy(
            src_ref=cot_ref.at[chunk_rows(chunk), columns(h)],
            dst_ref=cot.at[h, chunk_rows(chunk), :],
            send_sem=cot_send.at[h, chunk],
            recv_sem=cot_recv.at[h],
            device_id=partner,
            device_id_type=MESH,
        )

    def ctx_copy(h, chunk):
        return pltpu.make_async_remote_copy(
            src_ref=ctx.at[h, chunk_rows(chunk), :],
            dst_ref=context_ref.at[chunk_rows(chunk), columns(h)],
            send_sem=ctx_send.at[h, chunk],
            recv_sem=ctx_recv,
            device_id=partner,
            device_id_type=MESH,
        )

    def start_cot(h):
        def body(chunk, carry):
            cot_copy(h, chunk).start()
            return carry
        lax.fori_loop(0, N_CHUNK, body, 0)

    def start_in(step, carry):
        in_copy(step, 0).start()
        return carry

    for h in range(2):
        pltpu.make_async_copy(
            biased.at[my_seq, :, :, columns(my_head + h)], qkv.at[h, :, my_rows, :], in_recv.at[h]
        ).start()
    lax.fori_loop(1, N_SHARD, start_in, 0)

    @pl.when(section == 0)
    def _():
        pl.semaphore_wait(ready, N_Z)

    start_cot(0)

    def follow_in(step, carry):
        in_copy(step, 0).wait_send()
        in_copy(step, 1).start()
        return carry

    lax.fori_loop(1, N_SHARD, follow_in, 0)
    start_cot(1)

    part[...] = jnp.zeros_like(part)

    def rows_of(block):
        return pl.ds(pl.multiple_of(block * BLOCK, BLOCK), BLOCK)

    def stage_copy(src, dst, sends, recv, device):
        return pltpu.make_async_remote_copy(
            src_ref=src, dst_ref=dst, send_sem=sends, recv_sem=recv, device_id=device, device_id_type=MESH
        )

    def s1_copy(step):
        return stage_copy(part, stage1.at[dp], s1_send.at[step], s1_recv, dp_device(step))

    def s2_copy(step):
        return stage_copy(total, stage2.at[ring], s2_send.at[step], s2_recv, ring_device(step))

    def s3_copy(step):
        return stage_copy(pairs, stage3.at[inner], s3_send.at[step], s3_recv, plane_device(step))

    def begin(make, src, dst, recv, count):
        pltpu.make_async_copy(src, dst, recv).start()

        def body(step, carry):
            make(step).start()
            return carry
        lax.fori_loop(1, count, body, 0)

    def sent(make, count):
        def body(step, carry):
            make(step).wait_send()
            return carry
        lax.fori_loop(1, count, body, 0)

    def head_step(h, carry):
        pltpu.make_async_copy(qkv.at[h], qkv.at[h], in_recv.at[h]).wait()

        def turn(c, carry):
            k_t[:, rows_of(c)] = qkv[h, 1, rows_of(c), :].T
            v_t[:, rows_of(c)] = qkv[h, 2, rows_of(c), :].T
            return carry

        lax.fori_loop(0, N_BLOCK, turn, 0)
        dk_acc[...] = jnp.zeros_like(dk_acc)
        dv_acc[...] = jnp.zeros_like(dv_acc)
        pltpu.make_async_copy(cot.at[h], cot.at[h], cot_recv.at[h]).wait()

        def query_block(b, carry):
            query = qkv[h, 0, rows_of(b), :]
            grad_out = cot[h, rows_of(b), :]
            ctx_acc[...] = jnp.zeros_like(ctx_acc)
            dq_acc[...] = jnp.zeros_like(dq_acc)

            def scores_of(c):
                return lax.dot_general(
                    qkv[h, 1, rows_of(c), :], query, (((1,), (1,)), ((), ())),
                    preferred_element_type=jnp.float32,
                ) * scale

            def first(c, top):
                s = scores_of(c)
                score[rows_of(c), :] = s
                return jnp.maximum(top, jnp.max(s, axis=0, keepdims=True))

            top = lax.fori_loop(0, b, first, jnp.full((1, BLOCK), -jnp.inf, jnp.float32))
            s = scores_of(b)
            key_id = lax.broadcasted_iota(jnp.int32, s.shape, 0)
            query_id = lax.broadcasted_iota(jnp.int32, s.shape, 1)
            s = jnp.where(key_id <= query_id, s, -jnp.inf)
            score[rows_of(b), :] = s
            top = jnp.maximum(top, jnp.max(s, axis=0, keepdims=True))

            def second(c, denom):
                e = jnp.exp(score[rows_of(c), :] - top)
                score[rows_of(c), :] = e
                return denom + jnp.sum(e, axis=0, keepdims=True)

            denom = lax.fori_loop(0, b + 1, second, jnp.zeros((1, BLOCK), jnp.float32))
            inverse = 1.0 / denom

            def third(c, delta):
                probability = score[rows_of(c), :] * inverse
                weights = probability.astype(jnp.bfloat16)
                ctx_acc[...] += jnp.dot(v_t[:, rows_of(c)], weights, preferred_element_type=jnp.float32)
                dv_acc[rows_of(c), :] += jnp.dot(weights, grad_out, preferred_element_type=jnp.float32)
                grad_prob = lax.dot_general(
                    qkv[h, 2, rows_of(c), :], grad_out, (((1,), (1,)), ((), ())),
                    preferred_element_type=jnp.float32,
                )
                dprob[rows_of(c), :] = grad_prob
                return delta + jnp.sum(probability * grad_prob, axis=0, keepdims=True)

            delta = lax.fori_loop(0, b + 1, third, jnp.zeros((1, BLOCK), jnp.float32))

            def fourth(c, carry):
                probability = score[rows_of(c), :] * inverse
                grad_score = (probability * (dprob[rows_of(c), :] - delta) * scale).astype(jnp.bfloat16)
                dq_acc[...] += jnp.dot(k_t[:, rows_of(c)], grad_score, preferred_element_type=jnp.float32)
                dk_acc[rows_of(c), :] += jnp.dot(grad_score, query, preferred_element_type=jnp.float32)
                return carry

            lax.fori_loop(0, b + 1, fourth, 0)
            ctx[h, rows_of(b), :] = ctx_acc[...].T.astype(jnp.bfloat16)
            grads[h, 0, rows_of(b), :] = dq_acc[...].T.astype(jnp.bfloat16)
            for part_id in range(BLOCK // CHUNK):
                ctx_copy(h, b * (BLOCK // CHUNK) + part_id).start()
            return carry

        lax.fori_loop(0, N_BLOCK, query_block, 0)

        def finish(c, carry):
            dk = dk_acc[rows_of(c), :].astype(jnp.bfloat16)
            dv = dv_acc[rows_of(c), :].astype(jnp.bfloat16)
            grads[h, 1, rows_of(c), :] = dk
            grads[h, 2, rows_of(c), :] = dv
            dq = grads[h, 0, rows_of(c), :]
            return tuple(
                acc + jnp.sum(x.astype(jnp.float32), axis=0, keepdims=True)
                for acc, x in zip(carry, (dq, dk, dv))
            )

        sums = lax.fori_loop(0, N_BLOCK, finish, (jnp.zeros((1, HEAD_DIM), jnp.float32),) * 3)
        for kind in range(3):
            part[pl.ds(h * 3 + kind, 1), :] = sums[kind]

        @pl.when(h == 1)
        def _():
            begin(s1_copy, part, stage1.at[dp], s1_recv, N_DP)

        own = pltpu.make_async_copy(
            grads.at[h, :, my_rows, :], grad_ref.at[my_seq, :, :, columns(my_head + h)], out_recv
        )
        own.start()

        def start_out(step, carry):
            out_copy(step, h).start()
            return carry

        lax.fori_loop(1, SECOND_STAGE, start_out, 0)

        @pl.when(h == 1)
        def _():
            pltpu.make_async_copy(stage1, stage1, s1_recv).wait()
            total[...] = jnp.sum(stage1[...], axis=0)
            begin(s2_copy, total, stage2.at[ring], s2_recv, 2 * N_Z)

        lax.fori_loop(SECOND_STAGE, THIRD_STAGE, start_out, 0)

        @pl.when(h == 1)
        def _():
            pltpu.make_async_copy(stage2, stage2, s2_recv).wait()
            for odd in range(2):
                pairs[odd] = stage2[1 - odd] + stage2[3 - odd] + stage2[5 - odd] + stage2[7 - odd]
            begin(s3_copy, pairs, stage3.at[inner], s3_recv, LINE)

        lax.fori_loop(THIRD_STAGE, N_SHARD, start_out, 0)
        return carry

    lax.fori_loop(0, 2, head_step, 0)

    pltpu.make_async_copy(stage3, stage3, s3_recv).wait()
    for odd in range(2):
        for p in range(LINE):
            for h in range(2):
                first_column = ((odd * LINE + p) * 2 + h) * HEAD_DIM
                bias_grad_ref[:, first_column:first_column + HEAD_DIM] = stage3[p, odd, h * 3:h * 3 + 3, :]
    sent(s1_copy, N_DP)
    sent(s2_copy, 2 * N_Z)
    sent(s3_copy, LINE)

    def drain(step, carry):
        in_copy(step, 1).wait_send()
        out_copy(step, 0).wait_send()
        out_copy(step, 1).wait_send()
        return carry

    lax.fori_loop(1, N_SHARD, drain, 0)

    def drain_chunks(chunk, carry):
        for h in range(2):
            cot_copy(h, chunk).wait_send()
            ctx_copy(h, chunk).wait_send()
        return carry

    lax.fori_loop(0, N_CHUNK, drain_chunks, 0)
    pltpu.make_async_copy(context_ref, context_ref, ctx_recv).wait()
    pltpu.make_async_copy(grad_ref, grad_ref, out_recv).wait()


def per_device(projections, bias_terms, context_grad):
    proj = projections[0].transpose(0, 2, 1, 3)
    cot = context_grad.reshape(SEQ_LEN, 2 * HEAD_DIM)
    bf16, f32 = jnp.bfloat16, jnp.float32
    vmem = pl.BlockSpec(memory_space=pltpu.VMEM)
    anywhere = pl.BlockSpec(memory_space=pl.ANY)
    hbm = pl.BlockSpec(memory_space=pltpu.HBM)
    dma = pltpu.SemaphoreType.DMA
    context, grad, bias_grad = pl.pallas_call(
        kernel,
        out_shape=(
            jax.ShapeDtypeStruct((SEQ_LEN, 2 * HEAD_DIM), bf16),
            jax.ShapeDtypeStruct((2, 3, PIECE, WIDTH), bf16),
            jax.ShapeDtypeStruct((3, WIDTH), f32),
        ),
        in_specs=[hbm, hbm, hbm],
        out_specs=(anywhere, anywhere, vmem),
        scratch_shapes=[
            pltpu.VMEM((2, 3, PIECE, WIDTH), bf16),
            pltpu.VMEM((3, WIDTH), f32),
            pltpu.VMEM((2, 3, SEQ_LEN, HEAD_DIM), bf16),
            pltpu.VMEM((2, SEQ_LEN, HEAD_DIM), bf16),
            pltpu.VMEM((2, SEQ_LEN, HEAD_DIM), bf16),
            pltpu.VMEM((2, 3, SEQ_LEN, HEAD_DIM), bf16),
            pltpu.VMEM((SEQ_LEN, HEAD_DIM), f32),
            pltpu.VMEM((SEQ_LEN, HEAD_DIM), f32),
            pltpu.VMEM((HEAD_DIM, BLOCK), f32),
            pltpu.VMEM((HEAD_DIM, BLOCK), f32),
            pltpu.VMEM((SEQ_LEN, BLOCK), f32),
            pltpu.VMEM((SEQ_LEN, BLOCK), f32),
            pltpu.VMEM((HEAD_DIM, SEQ_LEN), bf16),
            pltpu.VMEM((HEAD_DIM, SEQ_LEN), bf16),
            pltpu.VMEM((8, HEAD_DIM), f32),
            pltpu.VMEM((8, HEAD_DIM), f32),
            pltpu.VMEM((2, 8, HEAD_DIM), f32),
            pltpu.VMEM((N_DP, 8, HEAD_DIM), f32),
            pltpu.VMEM((2 * N_Z, 8, HEAD_DIM), f32),
            pltpu.VMEM((LINE, 2, 8, HEAD_DIM), f32),
            dma((2, N_SHARD)), dma((2,)),
            dma((2, N_CHUNK)), dma((2,)),
            dma((2, N_SHARD)), dma,
            dma((2, N_CHUNK)), dma,
            dma((N_DP,)), dma,
            dma((2 * N_Z,)), dma,
            dma((LINE,)), dma,
            dma((2, 3)), dma,
            pltpu.SemaphoreType.REGULAR,
        ],
        compiler_params=pltpu.CompilerParams(
            collective_id=0, has_side_effects=True, vmem_limit_bytes=36 * 2**20
        ),
        cost_estimate=pl.CostEstimate(
            flops=8 * 10**9, bytes_accessed=10 * 2**20, transcendentals=5 * 10**6
        ),
    )(*(pltpu.with_memory_space_constraint(x, pltpu.HBM) for x in (proj, bias_terms, cot)))
    return (
        context.reshape(context_grad.shape),
        grad.transpose(0, 2, 1, 3)[None],
        bias_grad,
    )


def solution(mesh):
    placed = (
        P("section", "dp", "shard", None, None),
        P(),
        P("section", "dp", "shard", None, None, None),
    )
    return jax.shard_map(
        per_device,
        mesh=mesh,
        in_specs=placed,
        out_specs=(
            P("section", "dp", "shard", None, None, None),
            P("section", "dp", "shard", None, None),
            P(),
        ),
        check_vma=False,
    )
```

```python
import functools

import jax
import jax.numpy as jnp
from jax import lax
from jax.experimental import pallas as pl
from jax.experimental.pallas import tpu as pltpu
from jax.sharding import PartitionSpec as P

HEAD_DIM = 128
N_DP, N_Z, N_Y, N_CORE = 4, 4, 4, 2
N_SHARD = N_Z * N_Y * N_CORE
LINE = N_Y * N_CORE
PIECE = 64
SEQ_LEN = N_SHARD * PIECE
WIDTH = 4096
BLOCK = 512
SECOND_STAGE = 16
THIRD_STAGE = 26
CHUNK = 512
N_CHUNK = SEQ_LEN // CHUNK
N_BLOCK = SEQ_LEN // BLOCK
MESH = pl.DeviceIdType.MESH


def kernel(
    proj_ref, bias_hbm, cot_ref, context_ref, grad_ref, bias_grad_ref,
    biased, bias_ref, qkv, cot, ctx, grads, dk_acc, dv_acc, ctx_acc, dq_acc, score, dprob, k_t, v_t,
    part, total, pairs, stage1, stage2, stage3,
    in_send, in_recv, cot_send, cot_recv, out_send, out_recv, ctx_send, ctx_recv,
    s1_send, s1_recv, s2_send, s2_recv, s3_send, s3_recv, load_sem, bias_sem, ready,
):
    dp = lax.axis_index("dp")
    section = lax.axis_index("section")
    me = lax.axis_index("shard")
    z, inner = lax.div(me, LINE), lax.rem(me, LINE)
    y, core = lax.div(inner, N_CORE), lax.rem(inner, N_CORE)
    partner = (dp, 1 - section, (N_Z - 1 - z) * LINE + inner)
    scale = HEAD_DIM ** -0.5

    def split(value, by):
        if isinstance(value, int):
            return value // by, value % by
        return lax.div(value, by), lax.rem(value, by)

    def peer(step):
        rest, step_z = split(N_SHARD - step, N_Z)
        step_y, step_core = split(rest, N_CORE)
        to_z = lax.rem(z + step_z, N_Z)
        to_y = lax.rem(y + step_y, N_Y)
        to_core = lax.rem(core + step_core, N_CORE)
        return to_z * LINE + to_y * N_CORE + to_core

    def held_by(shard):
        shard_z, shard_inner = split(shard, LINE)
        home_z = N_Z - 1 - shard_z
        seq, odd = split(home_z, 2)
        return seq, (odd * LINE + shard_inner) * 2

    ring = section * N_Z + z

    def dp_device(step):
        return lax.rem(dp + step, N_DP), section, me

    def ring_device(step):
        to_section, to_z = split(lax.rem(ring + step, 2 * N_Z), N_Z)
        return dp, to_section, to_z * LINE + inner

    def plane_device(step):
        step_y, step_core = split(step, N_CORE)
        to_y = lax.rem(y + step_y, N_Y)
        to_core = lax.rem(core + step_core, N_CORE)
        return dp, section, z * LINE + to_y * N_CORE + to_core

    barrier = pltpu.get_barrier_semaphore()

    def tell(sem, device):
        pl.semaphore_signal(sem, inc=1, device_id=device, device_id_type=MESH)

    def other_section(h):
        return dp, 1 - section, h * LINE + inner

    for step in range(1, N_SHARD):
        tell(barrier, (dp, section, peer(step)))
    for step in range(1, N_DP):
        tell(barrier, dp_device(step))

    @pl.when(section == 0)
    def _():
        for far_z in range(N_Z):
            tell(barrier, other_section(far_z))

    def load(n, kind):
        return pltpu.make_async_copy(proj_ref.at[n, kind], biased.at[n, kind], load_sem.at[n, kind])

    load_bias = pltpu.make_async_copy(bias_hbm, bias_ref, bias_sem)
    load_bias.start()
    for n in range(2):
        for kind in range(3):
            load(n, kind).start()

    load_bias.wait()
    for n in range(2):
        for kind in range(3):
            load(n, kind).wait()
            biased[n, kind] = (
                biased[n, kind].astype(jnp.float32) + bias_ref[kind:kind + 1, :]
            ).astype(jnp.bfloat16)

    @pl.when(section == 0)
    def _():
        pl.semaphore_wait(barrier, N_SHARD - 1 + N_DP - 1)

    @pl.when(section == 1)
    def _():
        pl.semaphore_wait(barrier, N_SHARD - 1 + N_DP - 1 + N_Z)
        for far_z in range(N_Z):
            tell(ready, other_section(far_z))

    my_seq, my_head = held_by(me)
    my_rows = pl.ds(pl.multiple_of(me * PIECE, PIECE), PIECE)

    def columns(head):
        return pl.ds(pl.multiple_of(head * HEAD_DIM, HEAD_DIM), HEAD_DIM)

    def in_copy(step, h):
        to = peer(step)
        seq, head = held_by(to)
        return pltpu.make_async_remote_copy(
            src_ref=biased.at[seq, :, :, columns(head + h)],
            dst_ref=qkv.at[h, :, my_rows, :],
            send_sem=in_send.at[h, step],
            recv_sem=in_recv.at[h],
            device_id=(dp, section, to),
            device_id_type=MESH,
        )

    def out_copy(step, h):
        to = peer(step)
        rows = pl.ds(pl.multiple_of(to * PIECE, PIECE), PIECE)
        return pltpu.make_async_remote_copy(
            src_ref=grads.at[h, :, rows, :],
            dst_ref=grad_ref.at[my_seq, :, :, columns(my_head + h)],
            send_sem=out_send.at[h, step],
            recv_sem=out_recv,
            device_id=(dp, section, to),
            device_id_type=MESH,
        )

    def chunk_rows(chunk):
        return pl.ds(pl.multiple_of(chunk * CHUNK, CHUNK), CHUNK)

    def cot_copy(h, chunk):
        return pltpu.make_async_remote_copy(
            src_ref=cot_ref.at[chunk_rows(chunk), columns(h)],
            dst_ref=cot.at[h, chunk_rows(chunk), :],
            send_sem=cot_send.at[h, chunk],
            recv_sem=cot_recv.at[h],
            device_id=partner,
            device_id_type=MESH,
        )

    def ctx_copy(h, chunk):
        return pltpu.make_async_remote_copy(
            src_ref=ctx.at[h, chunk_rows(chunk), :],
            dst_ref=context_ref.at[chunk_rows(chunk), columns(h)],
            send_sem=ctx_send.at[h, chunk],
            recv_sem=ctx_recv,
            device_id=partner,
            device_id_type=MESH,
        )

    def start_cot(h):
        def body(chunk, carry):
            cot_copy(h, chunk).start()
            return carry
        lax.fori_loop(0, N_CHUNK, body, 0)

    def start_in(step, carry):
        in_copy(step, 0).start()
        return carry

    for h in range(2):
        pltpu.make_async_copy(
            biased.at[my_seq, :, :, columns(my_head + h)], qkv.at[h, :, my_rows, :], in_recv.at[h]
        ).start()
    lax.fori_loop(1, N_SHARD, start_in, 0)

    @pl.when(section == 0)
    def _():
        pl.semaphore_wait(ready, N_Z)

    start_cot(0)
    start_cot(1)

    def follow_in(step, carry):
        in_copy(step, 0).wait_send()
        in_copy(step, 1).start()
        return carry

    lax.fori_loop(1, N_SHARD, follow_in, 0)

    part[...] = jnp.zeros_like(part)

    def rows_of(block):
        return pl.ds(pl.multiple_of(block * BLOCK, BLOCK), BLOCK)

    def stage_copy(src, dst, sends, recv, device):
        return pltpu.make_async_remote_copy(
            src_ref=src, dst_ref=dst, send_sem=sends, recv_sem=recv, device_id=device, device_id_type=MESH
        )

    def s1_copy(step):
        return stage_copy(part, stage1.at[dp], s1_send.at[step], s1_recv, dp_device(step))

    def s2_copy(step):
        return stage_copy(total, stage2.at[ring], s2_send.at[step], s2_recv, ring_device(step))

    def s3_copy(step):
        return stage_copy(pairs, stage3.at[inner], s3_send.at[step], s3_recv, plane_device(step))

    def begin(make, src, dst, recv, count):
        pltpu.make_async_copy(src, dst, recv).start()

        def body(step, carry):
            make(step).start()
            return carry
        lax.fori_loop(1, count, body, 0)

    def sent(make, count):
        def body(step, carry):
            make(step).wait_send()
            return carry
        lax.fori_loop(1, count, body, 0)

    def head_step(h, carry):
        pltpu.make_async_copy(qkv.at[h], qkv.at[h], in_recv.at[h]).wait()

        def turn(c, carry):
            k_t[:, rows_of(c)] = qkv[h, 1, rows_of(c), :].T
            v_t[:, rows_of(c)] = qkv[h, 2, rows_of(c), :].T
            return carry

        lax.fori_loop(0, N_BLOCK, turn, 0)
        dk_acc[...] = jnp.zeros_like(dk_acc)
        dv_acc[...] = jnp.zeros_like(dv_acc)
        pltpu.make_async_copy(cot.at[h], cot.at[h], cot_recv.at[h]).wait()

        def query_block(b, carry):
            query = qkv[h, 0, rows_of(b), :]
            grad_out = cot[h, rows_of(b), :]
            ctx_acc[...] = jnp.zeros_like(ctx_acc)
            dq_acc[...] = jnp.zeros_like(dq_acc)

            def scores_of(c):
                return lax.dot_general(
                    qkv[h, 1, rows_of(c), :], query, (((1,), (1,)), ((), ())),
                    preferred_element_type=jnp.float32,
                ) * scale

            def first(c, top):
                s = scores_of(c)
                score[rows_of(c), :] = s
                return jnp.maximum(top, jnp.max(s, axis=0, keepdims=True))

            top = lax.fori_loop(0, b, first, jnp.full((1, BLOCK), -jnp.inf, jnp.float32))
            s = scores_of(b)
            key_id = lax.broadcasted_iota(jnp.int32, s.shape, 0)
            query_id = lax.broadcasted_iota(jnp.int32, s.shape, 1)
            s = jnp.where(key_id <= query_id, s, -jnp.inf)
            score[rows_of(b), :] = s
            top = jnp.maximum(top, jnp.max(s, axis=0, keepdims=True))

            def second(c, denom):
                e = jnp.exp(score[rows_of(c), :] - top)
                score[rows_of(c), :] = e
                return denom + jnp.sum(e, axis=0, keepdims=True)

            denom = lax.fori_loop(0, b + 1, second, jnp.zeros((1, BLOCK), jnp.float32))
            inverse = 1.0 / denom

            def third(c, delta):
                probability = score[rows_of(c), :] * inverse
                weights = probability.astype(jnp.bfloat16)
                ctx_acc[...] += jnp.dot(v_t[:, rows_of(c)], weights, preferred_element_type=jnp.float32)
                dv_acc[rows_of(c), :] += jnp.dot(weights, grad_out, preferred_element_type=jnp.float32)
                grad_prob = lax.dot_general(
                    qkv[h, 2, rows_of(c), :], grad_out, (((1,), (1,)), ((), ())),
                    preferred_element_type=jnp.float32,
                )
                dprob[rows_of(c), :] = grad_prob
                return delta + jnp.sum(probability * grad_prob, axis=0, keepdims=True)

            delta = lax.fori_loop(0, b + 1, third, jnp.zeros((1, BLOCK), jnp.float32))

            def fourth(c, carry):
                probability = score[rows_of(c), :] * inverse
                grad_score = (probability * (dprob[rows_of(c), :] - delta) * scale).astype(jnp.bfloat16)
                dq_acc[...] += jnp.dot(k_t[:, rows_of(c)], grad_score, preferred_element_type=jnp.float32)
                dk_acc[rows_of(c), :] += jnp.dot(grad_score, query, preferred_element_type=jnp.float32)
                return carry

            lax.fori_loop(0, b + 1, fourth, 0)
            ctx[h, rows_of(b), :] = ctx_acc[...].T.astype(jnp.bfloat16)
            grads[h, 0, rows_of(b), :] = dq_acc[...].T.astype(jnp.bfloat16)
            for part_id in range(BLOCK // CHUNK):
                ctx_copy(h, b * (BLOCK // CHUNK) + part_id).start()
            return carry

        lax.fori_loop(0, N_BLOCK, query_block, 0)

        def finish(c, carry):
            dk = dk_acc[rows_of(c), :].astype(jnp.bfloat16)
            dv = dv_acc[rows_of(c), :].astype(jnp.bfloat16)
            grads[h, 1, rows_of(c), :] = dk
            grads[h, 2, rows_of(c), :] = dv
            dq = grads[h, 0, rows_of(c), :]
            return tuple(
                acc + jnp.sum(x.astype(jnp.float32), axis=0, keepdims=True)
                for acc, x in zip(carry, (dq, dk, dv))
            )

        sums = lax.fori_loop(0, N_BLOCK, finish, (jnp.zeros((1, HEAD_DIM), jnp.float32),) * 3)
        for kind in range(3):
            part[pl.ds(h * 3 + kind, 1), :] = sums[kind]

        @pl.when(h == 1)
        def _():
            begin(s1_copy, part, stage1.at[dp], s1_recv, N_DP)

        own = pltpu.make_async_copy(
            grads.at[h, :, my_rows, :], grad_ref.at[my_seq, :, :, columns(my_head + h)], out_recv
        )
        own.start()

        def start_out(step, carry):
            out_copy(step, h).start()
            return carry

        lax.fori_loop(1, SECOND_STAGE, start_out, 0)

        @pl.when(h == 1)
        def _():
            pltpu.make_async_copy(stage1, stage1, s1_recv).wait()
            total[...] = jnp.sum(stage1[...], axis=0)
            begin(s2_copy, total, stage2.at[ring], s2_recv, 2 * N_Z)

        lax.fori_loop(SECOND_STAGE, THIRD_STAGE, start_out, 0)

        @pl.when(h == 1)
        def _():
            pltpu.make_async_copy(stage2, stage2, s2_recv).wait()
            for odd in range(2):
                pairs[odd] = stage2[1 - odd] + stage2[3 - odd] + stage2[5 - odd] + stage2[7 - odd]
            begin(s3_copy, pairs, stage3.at[inner], s3_recv, LINE)

        lax.fori_loop(THIRD_STAGE, N_SHARD, start_out, 0)
        return carry

    lax.fori_loop(0, 2, head_step, 0)

    pltpu.make_async_copy(stage3, stage3, s3_recv).wait()
    for odd in range(2):
        for p in range(LINE):
            for h in range(2):
                first_column = ((odd * LINE + p) * 2 + h) * HEAD_DIM
                bias_grad_ref[:, first_column:first_column + HEAD_DIM] = stage3[p, odd, h * 3:h * 3 + 3, :]
    sent(s1_copy, N_DP)
    sent(s2_copy, 2 * N_Z)
    sent(s3_copy, LINE)

    def drain(step, carry):
        in_copy(step, 1).wait_send()
        out_copy(step, 0).wait_send()
        out_copy(step, 1).wait_send()
        return carry

    lax.fori_loop(1, N_SHARD, drain, 0)

    def drain_chunks(chunk, carry):
        for h in range(2):
            cot_copy(h, chunk).wait_send()
            ctx_copy(h, chunk).wait_send()
        return carry

    lax.fori_loop(0, N_CHUNK, drain_chunks, 0)
    pltpu.make_async_copy(context_ref, context_ref, ctx_recv).wait()
    pltpu.make_async_copy(grad_ref, grad_ref, out_recv).wait()


def per_device(projections, bias_terms, context_grad):
    proj = projections[0].transpose(0, 2, 1, 3)
    cot = context_grad.reshape(SEQ_LEN, 2 * HEAD_DIM)
    bf16, f32 = jnp.bfloat16, jnp.float32
    vmem = pl.BlockSpec(memory_space=pltpu.VMEM)
    anywhere = pl.BlockSpec(memory_space=pl.ANY)
    hbm = pl.BlockSpec(memory_space=pltpu.HBM)
    dma = pltpu.SemaphoreType.DMA
    context, grad, bias_grad = pl.pallas_call(
        kernel,
        out_shape=(
            jax.ShapeDtypeStruct((SEQ_LEN, 2 * HEAD_DIM), bf16),
            jax.ShapeDtypeStruct((2, 3, PIECE, WIDTH), bf16),
            jax.ShapeDtypeStruct((3, WIDTH), f32),
        ),
        in_specs=[hbm, hbm, hbm],
        out_specs=(anywhere, anywhere, vmem),
        scratch_shapes=[
            pltpu.VMEM((2, 3, PIECE, WIDTH), bf16),
            pltpu.VMEM((3, WIDTH), f32),
            pltpu.VMEM((2, 3, SEQ_LEN, HEAD_DIM), bf16),
            pltpu.VMEM((2, SEQ_LEN, HEAD_DIM), bf16),
            pltpu.VMEM((2, SEQ_LEN, HEAD_DIM), bf16),
            pltpu.VMEM((2, 3, SEQ_LEN, HEAD_DIM), bf16),
            pltpu.VMEM((SEQ_LEN, HEAD_DIM), f32),
            pltpu.VMEM((SEQ_LEN, HEAD_DIM), f32),
            pltpu.VMEM((HEAD_DIM, BLOCK), f32),
            pltpu.VMEM((HEAD_DIM, BLOCK), f32),
            pltpu.VMEM((SEQ_LEN, BLOCK), f32),
            pltpu.VMEM((SEQ_LEN, BLOCK), f32),
            pltpu.VMEM((HEAD_DIM, SEQ_LEN), bf16),
            pltpu.VMEM((HEAD_DIM, SEQ_LEN), bf16),
            pltpu.VMEM((8, HEAD_DIM), f32),
            pltpu.VMEM((8, HEAD_DIM), f32),
            pltpu.VMEM((2, 8, HEAD_DIM), f32),
            pltpu.VMEM((N_DP, 8, HEAD_DIM), f32),
            pltpu.VMEM((2 * N_Z, 8, HEAD_DIM), f32),
            pltpu.VMEM((LINE, 2, 8, HEAD_DIM), f32),
            dma((2, N_SHARD)), dma((2,)),
            dma((2, N_CHUNK)), dma((2,)),
            dma((2, N_SHARD)), dma,
            dma((2, N_CHUNK)), dma,
            dma((N_DP,)), dma,
            dma((2 * N_Z,)), dma,
            dma((LINE,)), dma,
            dma((2, 3)), dma,
            pltpu.SemaphoreType.REGULAR,
        ],
        compiler_params=pltpu.CompilerParams(
            collective_id=0, has_side_effects=True, vmem_limit_bytes=36 * 2**20
        ),
        cost_estimate=pl.CostEstimate(
            flops=8 * 10**9, bytes_accessed=10 * 2**20, transcendentals=5 * 10**6
        ),
    )(*(pltpu.with_memory_space_constraint(x, pltpu.HBM) for x in (proj, bias_terms, cot)))
    return (
        context.reshape(context_grad.shape),
        grad.transpose(0, 2, 1, 3)[None],
        bias_grad,
    )


def solution(mesh):
    placed = (
        P("section", "dp", "shard", None, None),
        P(),
        P("section", "dp", "shard", None, None, None),
    )
    return jax.shard_map(
        per_device,
        mesh=mesh,
        in_specs=placed,
        out_specs=(
            P("section", "dp", "shard", None, None, None),
            P("section", "dp", "shard", None, None),
            P(),
        ),
        check_vma=False,
    )
```

```python
import functools

import jax
import jax.numpy as jnp
from jax import lax
from jax.experimental import pallas as pl
from jax.experimental.pallas import tpu as pltpu
from jax.sharding import PartitionSpec as P

HEAD_DIM = 128
N_DP, N_Z, N_Y, N_CORE = 4, 4, 4, 2
N_SHARD = N_Z * N_Y * N_CORE
LINE = N_Y * N_CORE
PIECE = 64
SEQ_LEN = N_SHARD * PIECE
WIDTH = 4096
BLOCK = 512
SECOND_STAGE = 12
THIRD_STAGE = 24
CHUNK = 512
N_CHUNK = SEQ_LEN // CHUNK
N_BLOCK = SEQ_LEN // BLOCK
MESH = pl.DeviceIdType.MESH


def kernel(
    proj_ref, bias_hbm, cot_ref, context_ref, grad_ref, bias_grad_ref,
    biased, bias_ref, qkv, cot, ctx, grads, dk_acc, dv_acc, ctx_acc, dq_acc, score, dprob, k_t, v_t,
    part, total, pairs, stage1, stage2, stage3,
    in_send, in_recv, cot_send, cot_recv, out_send, out_recv, ctx_send, ctx_recv,
    s1_send, s1_recv, s2_send, s2_recv, s3_send, s3_recv, load_sem, bias_sem, ready,
):
    dp = lax.axis_index("dp")
    section = lax.axis_index("section")
    me = lax.axis_index("shard")
    z, inner = lax.div(me, LINE), lax.rem(me, LINE)
    y, core = lax.div(inner, N_CORE), lax.rem(inner, N_CORE)
    partner = (dp, 1 - section, (N_Z - 1 - z) * LINE + inner)
    scale = HEAD_DIM ** -0.5

    def split(value, by):
        if isinstance(value, int):
            return value // by, value % by
        return lax.div(value, by), lax.rem(value, by)

    def peer(step):
        rest, step_z = split(N_SHARD - step, N_Z)
        step_y, step_core = split(rest, N_CORE)
        to_z = lax.rem(z + step_z, N_Z)
        to_y = lax.rem(y + step_y, N_Y)
        to_core = lax.rem(core + step_core, N_CORE)
        return to_z * LINE + to_y * N_CORE + to_core

    def held_by(shard):
        shard_z, shard_inner = split(shard, LINE)
        home_z = N_Z - 1 - shard_z
        seq, odd = split(home_z, 2)
        return seq, (odd * LINE + shard_inner) * 2

    ring = section * N_Z + z

    def dp_device(step):
        return lax.rem(dp + step, N_DP), section, me

    def ring_device(step):
        to_section, to_z = split(lax.rem(ring + step, 2 * N_Z), N_Z)
        return dp, to_section, to_z * LINE + inner

    def plane_device(step):
        step_y, step_core = split(step, N_CORE)
        to_y = lax.rem(y + step_y, N_Y)
        to_core = lax.rem(core + step_core, N_CORE)
        return dp, section, z * LINE + to_y * N_CORE + to_core

    barrier = pltpu.get_barrier_semaphore()

    def tell(sem, device):
        pl.semaphore_signal(sem, inc=1, device_id=device, device_id_type=MESH)

    def other_section(h):
        return dp, 1 - section, h * LINE + inner

    for step in range(1, N_SHARD):
        tell(barrier, (dp, section, peer(step)))
    for step in range(1, N_DP):
        tell(barrier, dp_device(step))

    @pl.when(section == 0)
    def _():
        for far_z in range(N_Z):
            tell(barrier, other_section(far_z))

    def load(n, kind):
        return pltpu.make_async_copy(proj_ref.at[n, kind], biased.at[n, kind], load_sem.at[n, kind])

    load_bias = pltpu.make_async_copy(bias_hbm, bias_ref, bias_sem)
    load_bias.start()
    for n in range(2):
        for kind in range(3):
            load(n, kind).start()

    load_bias.wait()
    for n in range(2):
        for kind in range(3):
            load(n, kind).wait()
            biased[n, kind] = (
                biased[n, kind].astype(jnp.float32) + bias_ref[kind:kind + 1, :]
            ).astype(jnp.bfloat16)

    @pl.when(section == 0)
    def _():
        pl.semaphore_wait(barrier, N_SHARD - 1 + N_DP - 1)

    @pl.when(section == 1)
    def _():
        pl.semaphore_wait(barrier, N_SHARD - 1 + N_DP - 1 + N_Z)
        for far_z in range(N_Z):
            tell(ready, other_section(far_z))

    my_seq, my_head = held_by(me)
    my_rows = pl.ds(pl.multiple_of(me * PIECE, PIECE), PIECE)

    def columns(head):
        return pl.ds(pl.multiple_of(head * HEAD_DIM, HEAD_DIM), HEAD_DIM)

    def in_copy(step, h):
        to = peer(step)
        seq, head = held_by(to)
        return pltpu.make_async_remote_copy(
            src_ref=biased.at[seq, :, :, columns(head + h)],
            dst_ref=qkv.at[h, :, my_rows, :],
            send_sem=in_send.at[h, step],
            recv_sem=in_recv.at[h],
            device_id=(dp, section, to),
            device_id_type=MESH,
        )

    def out_copy(step, h):
        to = peer(step)
        rows = pl.ds(pl.multiple_of(to * PIECE, PIECE), PIECE)
        return pltpu.make_async_remote_copy(
            src_ref=grads.at[h, :, rows, :],
            dst_ref=grad_ref.at[my_seq, :, :, columns(my_head + h)],
            send_sem=out_send.at[h, step],
            recv_sem=out_recv,
            device_id=(dp, section, to),
            device_id_type=MESH,
        )

    def chunk_rows(chunk):
        return pl.ds(pl.multiple_of(chunk * CHUNK, CHUNK), CHUNK)

    def cot_copy(h, chunk):
        return pltpu.make_async_remote_copy(
            src_ref=cot_ref.at[chunk_rows(chunk), columns(h)],
            dst_ref=cot.at[h, chunk_rows(chunk), :],
            send_sem=cot_send.at[h, chunk],
            recv_sem=cot_recv.at[h],
            device_id=partner,
            device_id_type=MESH,
        )

    def ctx_copy(h, chunk):
        return pltpu.make_async_remote_copy(
            src_ref=ctx.at[h, chunk_rows(chunk), :],
            dst_ref=context_ref.at[chunk_rows(chunk), columns(h)],
            send_sem=ctx_send.at[h, chunk],
            recv_sem=ctx_recv,
            device_id=partner,
            device_id_type=MESH,
        )

    def start_cot(h):
        def body(chunk, carry):
            cot_copy(h, chunk).start()
            return carry
        lax.fori_loop(0, N_CHUNK, body, 0)

    def start_in(step, carry):
        in_copy(step, 0).start()
        return carry

    for h in range(2):
        pltpu.make_async_copy(
            biased.at[my_seq, :, :, columns(my_head + h)], qkv.at[h, :, my_rows, :], in_recv.at[h]
        ).start()
    lax.fori_loop(1, N_SHARD, start_in, 0)

    @pl.when(section == 0)
    def _():
        pl.semaphore_wait(ready, N_Z)

    start_cot(0)
    start_cot(1)

    def follow_in(step, carry):
        in_copy(step, 0).wait_send()
        in_copy(step, 1).start()
        return carry

    lax.fori_loop(1, N_SHARD, follow_in, 0)

    part[...] = jnp.zeros_like(part)

    def rows_of(block):
        return pl.ds(pl.multiple_of(block * BLOCK, BLOCK), BLOCK)

    def stage_copy(src, dst, sends, recv, device):
        return pltpu.make_async_remote_copy(
            src_ref=src, dst_ref=dst, send_sem=sends, recv_sem=recv, device_id=device, device_id_type=MESH
        )

    def s1_copy(step):
        return stage_copy(part, stage1.at[dp], s1_send.at[step], s1_recv, dp_device(step))

    def s2_copy(step):
        return stage_copy(total, stage2.at[ring], s2_send.at[step], s2_recv, ring_device(step))

    def s3_copy(step):
        return stage_copy(pairs, stage3.at[inner], s3_send.at[step], s3_recv, plane_device(step))

    def begin(make, src, dst, recv, count):
        pltpu.make_async_copy(src, dst, recv).start()

        def body(step, carry):
            make(step).start()
            return carry
        lax.fori_loop(1, count, body, 0)

    def sent(make, count):
        def body(step, carry):
            make(step).wait_send()
            return carry
        lax.fori_loop(1, count, body, 0)

    def head_step(h, carry):
        pltpu.make_async_copy(qkv.at[h], qkv.at[h], in_recv.at[h]).wait()

        def turn(c, carry):
            k_t[:, rows_of(c)] = qkv[h, 1, rows_of(c), :].T
            v_t[:, rows_of(c)] = qkv[h, 2, rows_of(c), :].T
            return carry

        lax.fori_loop(0, N_BLOCK, turn, 0)
        dk_acc[...] = jnp.zeros_like(dk_acc)
        dv_acc[...] = jnp.zeros_like(dv_acc)
        pltpu.make_async_copy(cot.at[h], cot.at[h], cot_recv.at[h]).wait()

        def query_block(b, carry):
            query = qkv[h, 0, rows_of(b), :]
            grad_out = cot[h, rows_of(b), :]
            ctx_acc[...] = jnp.zeros_like(ctx_acc)
            dq_acc[...] = jnp.zeros_like(dq_acc)

            def scores_of(c):
                return lax.dot_general(
                    qkv[h, 1, rows_of(c), :], query, (((1,), (1,)), ((), ())),
                    preferred_element_type=jnp.float32,
                ) * scale

            def first(c, top):
                s = scores_of(c)
                score[rows_of(c), :] = s
                return jnp.maximum(top, jnp.max(s, axis=0, keepdims=True))

            top = lax.fori_loop(0, b, first, jnp.full((1, BLOCK), -jnp.inf, jnp.float32))
            s = scores_of(b)
            key_id = lax.broadcasted_iota(jnp.int32, s.shape, 0)
            query_id = lax.broadcasted_iota(jnp.int32, s.shape, 1)
            s = jnp.where(key_id <= query_id, s, -jnp.inf)
            score[rows_of(b), :] = s
            top = jnp.maximum(top, jnp.max(s, axis=0, keepdims=True))

            def second(c, denom):
                e = jnp.exp(score[rows_of(c), :] - top)
                score[rows_of(c), :] = e
                return denom + jnp.sum(e, axis=0, keepdims=True)

            denom = lax.fori_loop(0, b + 1, second, jnp.zeros((1, BLOCK), jnp.float32))
            inverse = 1.0 / denom

            def third(c, delta):
                probability = score[rows_of(c), :] * inverse
                weights = probability.astype(jnp.bfloat16)
                ctx_acc[...] += jnp.dot(v_t[:, rows_of(c)], weights, preferred_element_type=jnp.float32)
                dv_acc[rows_of(c), :] += jnp.dot(weights, grad_out, preferred_element_type=jnp.float32)
                grad_prob = lax.dot_general(
                    qkv[h, 2, rows_of(c), :], grad_out, (((1,), (1,)), ((), ())),
                    preferred_element_type=jnp.float32,
                )
                dprob[rows_of(c), :] = grad_prob
                return delta + jnp.sum(probability * grad_prob, axis=0, keepdims=True)

            delta = lax.fori_loop(0, b + 1, third, jnp.zeros((1, BLOCK), jnp.float32))

            def fourth(c, carry):
                probability = score[rows_of(c), :] * inverse
                grad_score = (probability * (dprob[rows_of(c), :] - delta) * scale).astype(jnp.bfloat16)
                dq_acc[...] += jnp.dot(k_t[:, rows_of(c)], grad_score, preferred_element_type=jnp.float32)
                dk_acc[rows_of(c), :] += jnp.dot(grad_score, query, preferred_element_type=jnp.float32)
                return carry

            lax.fori_loop(0, b + 1, fourth, 0)
            ctx[h, rows_of(b), :] = ctx_acc[...].T.astype(jnp.bfloat16)
            grads[h, 0, rows_of(b), :] = dq_acc[...].T.astype(jnp.bfloat16)
            for part_id in range(BLOCK // CHUNK):
                ctx_copy(h, b * (BLOCK // CHUNK) + part_id).start()
            return carry

        lax.fori_loop(0, N_BLOCK, query_block, 0)

        def finish(c, carry):
            dk = dk_acc[rows_of(c), :].astype(jnp.bfloat16)
            dv = dv_acc[rows_of(c), :].astype(jnp.bfloat16)
            grads[h, 1, rows_of(c), :] = dk
            grads[h, 2, rows_of(c), :] = dv
            dq = grads[h, 0, rows_of(c), :]
            return tuple(
                acc + jnp.sum(x.astype(jnp.float32), axis=0, keepdims=True)
                for acc, x in zip(carry, (dq, dk, dv))
            )

        sums = lax.fori_loop(0, N_BLOCK, finish, (jnp.zeros((1, HEAD_DIM), jnp.float32),) * 3)
        for kind in range(3):
            part[pl.ds(h * 3 + kind, 1), :] = sums[kind]

        @pl.when(h == 1)
        def _():
            begin(s1_copy, part, stage1.at[dp], s1_recv, N_DP)

        own = pltpu.make_async_copy(
            grads.at[h, :, my_rows, :], grad_ref.at[my_seq, :, :, columns(my_head + h)], out_recv
        )
        own.start()

        def start_out(step, carry):
            out_copy(step, h).start()
            return carry

        lax.fori_loop(1, SECOND_STAGE, start_out, 0)

        @pl.when(h == 1)
        def _():
            pltpu.make_async_copy(stage1, stage1, s1_recv).wait()
            total[...] = jnp.sum(stage1[...], axis=0)
            begin(s2_copy, total, stage2.at[ring], s2_recv, 2 * N_Z)

        lax.fori_loop(SECOND_STAGE, THIRD_STAGE, start_out, 0)

        @pl.when(h == 1)
        def _():
            pltpu.make_async_copy(stage2, stage2, s2_recv).wait()
            for odd in range(2):
                pairs[odd] = stage2[1 - odd] + stage2[3 - odd] + stage2[5 - odd] + stage2[7 - odd]
            begin(s3_copy, pairs, stage3.at[inner], s3_recv, LINE)

        lax.fori_loop(THIRD_STAGE, N_SHARD, start_out, 0)
        return carry

    lax.fori_loop(0, 2, head_step, 0)

    pltpu.make_async_copy(stage3, stage3, s3_recv).wait()
    for odd in range(2):
        for p in range(LINE):
            for h in range(2):
                first_column = ((odd * LINE + p) * 2 + h) * HEAD_DIM
                bias_grad_ref[:, first_column:first_column + HEAD_DIM] = stage3[p, odd, h * 3:h * 3 + 3, :]
    sent(s1_copy, N_DP)
    sent(s2_copy, 2 * N_Z)
    sent(s3_copy, LINE)

    def drain(step, carry):
        in_copy(step, 1).wait_send()
        out_copy(step, 0).wait_send()
        out_copy(step, 1).wait_send()
        return carry

    lax.fori_loop(1, N_SHARD, drain, 0)

    def drain_chunks(chunk, carry):
        for h in range(2):
            cot_copy(h, chunk).wait_send()
            ctx_copy(h, chunk).wait_send()
        return carry

    lax.fori_loop(0, N_CHUNK, drain_chunks, 0)
    pltpu.make_async_copy(context_ref, context_ref, ctx_recv).wait()
    pltpu.make_async_copy(grad_ref, grad_ref, out_recv).wait()


def per_device(projections, bias_terms, context_grad):
    proj = projections[0].transpose(0, 2, 1, 3)
    cot = context_grad.reshape(SEQ_LEN, 2 * HEAD_DIM)
    bf16, f32 = jnp.bfloat16, jnp.float32
    vmem = pl.BlockSpec(memory_space=pltpu.VMEM)
    anywhere = pl.BlockSpec(memory_space=pl.ANY)
    hbm = pl.BlockSpec(memory_space=pltpu.HBM)
    dma = pltpu.SemaphoreType.DMA
    context, grad, bias_grad = pl.pallas_call(
        kernel,
        out_shape=(
            jax.ShapeDtypeStruct((SEQ_LEN, 2 * HEAD_DIM), bf16),
            jax.ShapeDtypeStruct((2, 3, PIECE, WIDTH), bf16),
            jax.ShapeDtypeStruct((3, WIDTH), f32),
        ),
        in_specs=[hbm, hbm, hbm],
        out_specs=(anywhere, anywhere, vmem),
        scratch_shapes=[
            pltpu.VMEM((2, 3, PIECE, WIDTH), bf16),
            pltpu.VMEM((3, WIDTH), f32),
            pltpu.VMEM((2, 3, SEQ_LEN, HEAD_DIM), bf16),
            pltpu.VMEM((2, SEQ_LEN, HEAD_DIM), bf16),
            pltpu.VMEM((2, SEQ_LEN, HEAD_DIM), bf16),
            pltpu.VMEM((2, 3, SEQ_LEN, HEAD_DIM), bf16),
            pltpu.VMEM((SEQ_LEN, HEAD_DIM), f32),
            pltpu.VMEM((SEQ_LEN, HEAD_DIM), f32),
            pltpu.VMEM((HEAD_DIM, BLOCK), f32),
            pltpu.VMEM((HEAD_DIM, BLOCK), f32),
            pltpu.VMEM((SEQ_LEN, BLOCK), f32),
            pltpu.VMEM((SEQ_LEN, BLOCK), f32),
            pltpu.VMEM((HEAD_DIM, SEQ_LEN), bf16),
            pltpu.VMEM((HEAD_DIM, SEQ_LEN), bf16),
            pltpu.VMEM((8, HEAD_DIM), f32),
            pltpu.VMEM((8, HEAD_DIM), f32),
            pltpu.VMEM((2, 8, HEAD_DIM), f32),
            pltpu.VMEM((N_DP, 8, HEAD_DIM), f32),
            pltpu.VMEM((2 * N_Z, 8, HEAD_DIM), f32),
            pltpu.VMEM((LINE, 2, 8, HEAD_DIM), f32),
            dma((2, N_SHARD)), dma((2,)),
            dma((2, N_CHUNK)), dma((2,)),
            dma((2, N_SHARD)), dma,
            dma((2, N_CHUNK)), dma,
            dma((N_DP,)), dma,
            dma((2 * N_Z,)), dma,
            dma((LINE,)), dma,
            dma((2, 3)), dma,
            pltpu.SemaphoreType.REGULAR,
        ],
        compiler_params=pltpu.CompilerParams(
            collective_id=0, has_side_effects=True, vmem_limit_bytes=36 * 2**20
        ),
        cost_estimate=pl.CostEstimate(
            flops=8 * 10**9, bytes_accessed=10 * 2**20, transcendentals=5 * 10**6
        ),
    )(*(pltpu.with_memory_space_constraint(x, pltpu.HBM) for x in (proj, bias_terms, cot)))
    return (
        context.reshape(context_grad.shape),
        grad.transpose(0, 2, 1, 3)[None],
        bias_grad,
    )


def solution(mesh):
    placed = (
        P("section", "dp", "shard", None, None),
        P(),
        P("section", "dp", "shard", None, None, None),
    )
    return jax.shard_map(
        per_device,
        mesh=mesh,
        in_specs=placed,
        out_specs=(
            P("section", "dp", "shard", None, None, None),
            P("section", "dp", "shard", None, None),
            P(),
        ),
        check_vma=False,
    )
```
